512 devices in a mesh: rows: 32 (over z_hi, x, core), cols: 16 (over y, z_lo).
Axes of the slice: x: 4, y: 8, z: 8 (z_hi: 4, z_lo: 2; z = z_hi * 2 + z_lo), core: 2. Of those that a mesh axis runs over, the one named last changes fastest.
Arguments:
- tokens: bfloat16 [416, 2048], P(None, 'rows'), may hold values from -24 to 24
- arrival: int32 [416], replicated, may hold values from 0 to 415, each once
- cache_lengths: int32 [416], replicated, may hold values from 1 to 1023, as said below
- move_slot: int32 [32, 4], replicated, may hold values from 0 to 12, as said below
- move_target: int32 [32, 4], replicated, may hold values from 0 to 31, as said below
- page_table: int32 [32, 16, 13, 2], P('rows', 'cols'), may hold values from 0 to 25, as said below
- kv_pool: bfloat16 [832, 16, 32, 512], P('rows', 'cols'), may hold values from -400 to 400
- ssm_state: bfloat16 [416, 32, 64, 256], P('rows', 'cols'), may hold values from -1.5 to 1.5
- conv_x: bfloat16 [416, 3, 2048], P('rows', None, 'cols'), may hold values from -6 to 6
- conv_bc: bfloat16 [416, 3, 512], P('rows'), may hold values from -6 to 6
- norm_gain: bfloat16 [2048], P('rows'), may hold values from 0.099609375 to 1.8984375
- weight_z: bfloat16 [2048, 2048], P('rows', 'cols'), may hold values from -0.125 to 0.125
- weight_x: bfloat16 [2048, 2048], P('rows', 'cols'), may hold values from -0.125 to 0.125
- weight_dt: bfloat16 [2048, 32], P('rows', 'cols'), may hold values from -0.125 to 0.125
- weight_bc: bfloat16 [2048, 512], P('rows'), may hold values from -0.125 to 0.125
- weight_qkv: bfloat16 [2048, 1536], P('rows'), may hold values from -0.125 to 0.125
- conv_weight_x: bfloat16 [4, 2048], P(None, 'cols'), may hold values from -3 to 3
- conv_weight_bc: bfloat16 [4, 512], replicated, may hold values from -3 to 3
- dt_bias: float32 [32], P('cols'), may hold values from -4 to -1
- a_log: float32 [32], P('cols'), may hold values from 0 to 2.5
- d_skip: float32 [32], P('cols'), may hold values from 0.5 to 1.5
- weight_ssm_out: bfloat16 [2048, 2048], P('cols'), may hold values from -0.125 to 0.125
- weight_attn_out: bfloat16 [1024, 2048], P('cols'), may hold values from -0.1875 to 0.1875
Outputs:
- mixed: bfloat16 [416, 2048], P('rows', 'cols')
- ssm_next: bfloat16 [416, 32, 64, 256], P('rows', 'cols')
- conv_x_next: bfloat16 [416, 3, 2048], P('rows', None, 'cols')
- conv_bc_next: bfloat16 [416, 3, 512], P('rows')
- kv_next: bfloat16 [832, 16, 32, 512], P('rows', 'cols')
The draws below stay inside these ranges and needn't reach their ends.
Inputs may be any that keep to these rules, and one draw needn't show every extreme that they name: `cache_lengths`: some request has 1023 cached tokens. `move_slot`: each row lists 4 distinct slots. `move_target`: each row lists 4 distinct row indices other than its own; every row index is named exactly 4 times, by distinct sources. `page_table`: the 13 x 2 entries of one device are each of 0 to 25 once.
All inputs are finite; a program needn't handle non-finite values.
Results may differ from the reference program's by a relative error of at most 0.011.
Values may be sent and summed in bfloat16 or wider, within the bound.
A program may use at most 64 MiB of HBM per device.

```python
import jax
import jax.numpy as jnp
from jax import lax

D = 2048
NH = 32
HP = 64
NS = 256
KW = 4
QH = 8
KVH = 2
HD = 128
CTX = 1024
PAGE = 32
SLOTS = 13
DI = 2048
QKV = 1536
REQUESTS = 416
MIG = 4
PPD = 2
POOL = 26
N_ROWS = 32
N_COLS = 16


def draw_tokens(key, part):
    features = jnp.arange(D, dtype=jnp.float32) / D
    feature_scale = 0.5 + features
    values = jax.random.normal(key, (REQUESTS, D), jnp.float32) * feature_scale[None, :]
    return jnp.clip(values, -24.0, 24.0).astype(jnp.bfloat16)


def draw_cache_lengths(key, part):
    first_key, second_key, third_key = jax.random.split(jax.random.fold_in(key, 3), 3)
    first_draw = jax.random.randint(first_key, (REQUESTS,), 1, CTX)
    second_draw = jax.random.randint(second_key, (REQUESTS,), 1, CTX)
    shorter = jnp.minimum(first_draw, second_draw)
    longest = jax.random.randint(third_key, (), 0, REQUESTS)
    return jnp.where(jnp.arange(REQUESTS) == longest, CTX - 1, shorter).astype(jnp.int32)


def move_tables(key):
    base_key = jax.random.fold_in(key, 7)
    first_key, second_key, third_key = jax.random.split(base_key, 3)
    device_order = jax.random.permutation(first_key, N_ROWS)
    position = jnp.zeros((N_ROWS,), jnp.int32).at[device_order].set(jnp.arange(N_ROWS, dtype=jnp.int32))
    offsets = 1 + jax.random.permutation(second_key, N_ROWS - 1)[:MIG]
    targets = device_order[(position[:, None] + offsets[None, :]) % N_ROWS]
    scores = jax.random.randint(third_key, (N_ROWS, SLOTS), 0, 1 << 20) * SLOTS + jnp.arange(SLOTS)[None, :]
    leaving = jnp.argsort(scores, axis=1)[:, :MIG]
    return (leaving.astype(jnp.int32), targets.astype(jnp.int32))


def draw_move_slot(key, part):
    return move_tables(key)[0]


def draw_move_target(key, part):
    return move_tables(key)[1]


def draw_page_table(key, part):
    scores = jax.random.randint(jax.random.fold_in(key, 11), (N_ROWS, N_COLS, POOL), 0, 1 << 20) * POOL + jnp.arange(POOL)[None, None, :]
    ordering = jnp.argsort(scores, axis=2)
    return ordering.reshape(N_ROWS, N_COLS, SLOTS, PPD).astype(jnp.int32)


def draw_kv_pool(key, part):
    shape = (N_ROWS * POOL, N_COLS, PAGE, 2 * KVH * HD)
    first_key = jax.random.fold_in(jax.random.fold_in(key, 13), 0)
    noise = jax.random.normal(first_key, shape, jnp.float32)
    return jnp.clip(noise, -400.0, 400.0).astype(jnp.bfloat16)


def steps_of(stream_key, extent, cuts, low, top_value):
    def one(dim, shards_of):
        steps = jax.random.uniform(jax.random.fold_in(jax.random.fold_in(stream_key, 6), dim), (shards_of,), jnp.float32, low / len(cuts), top_value / len(cuts))
        return jnp.repeat(jnp.exp(steps), extent[dim] // shards_of).reshape((-1,) + (1,) * (len(extent) - dim - 1))

    loudness = one(*cuts[0])
    for cut in cuts[1:]:
        loudness = loudness * one(*cut)
    return loudness


def scatter_about(key, dims, spread, most, shards=(), kind=jnp.bfloat16):
    gain = steps_of(key, dims, shards, -0.22, 0.18) if shards else 1.0
    result = jax.random.normal(key, dims, jnp.float32) * spread * gain
    return jnp.minimum(jnp.maximum(result, -most), most).astype(kind)


def setup_inputs(seed: int = 0) -> dict:
    key_of = jax.random.split(jax.random.key(seed), 24)
    tokens = draw_tokens(jax.random.fold_in(key_of[23], 71), 0)
    arrival = jax.random.permutation(key_of[1], REQUESTS).astype(jnp.int32)
    cache_lengths = draw_cache_lengths(jax.random.fold_in(key_of[23], 71), 0)
    move_slot = draw_move_slot(jax.random.fold_in(key_of[23], 71), 0)
    move_target = draw_move_target(jax.random.fold_in(key_of[23], 71), 0)
    page_table = draw_page_table(jax.random.fold_in(key_of[23], 71), 0)
    kv_pool = draw_kv_pool(jax.random.fold_in(key_of[23], 71), 0)
    ssm_state = scatter_about(key_of[7], (REQUESTS, NH, HP, NS), 0.25, 1.5, ((0, 32), (1, 16)))
    conv_x = scatter_about(key_of[8], (REQUESTS, KW - 1, DI), 1.0, 6.0, ((0, 32), (2, 16)))
    conv_bc = scatter_about(key_of[9], (REQUESTS, KW - 1, 2 * NS), 1.0, 6.0, ((0, 32),))
    norm_gain = jnp.clip(1.0 + 0.18 * jax.random.normal(key_of[10], (D,), jnp.float32), 0.099609375, 1.8984375).astype(jnp.bfloat16)
    weight_z = scatter_about(key_of[11], (D, DI), D ** -0.5, 0.125, ((0, 32), (1, 16)))
    weight_x = scatter_about(key_of[12], (D, DI), D ** -0.5, 0.125, ((0, 32), (1, 16)))
    weight_dt = scatter_about(key_of[13], (D, NH), D ** -0.5, 0.125, ((0, 32), (1, 16)))
    weight_bc = scatter_about(key_of[14], (D, 2 * NS), D ** -0.5, 0.125, ((0, 32),))
    weight_qkv = scatter_about(key_of[15], (D, QKV), D ** -0.5, 0.125, ((0, 32),))
    conv_weight_x = scatter_about(key_of[16], (KW, DI), KW ** -0.5, 3.0, ((1, 16),))
    conv_weight_bc = scatter_about(key_of[17], (KW, 2 * NS), KW ** -0.5, 3.0)
    dt_bias = jnp.clip(-4.0 + 3.0 * jax.random.uniform(key_of[18], (NH,), jnp.float32) ** steps_of(key_of[18], (NH,), ((0, 16),), -0.2, 0.2), -4.0, -1.0)
    a_log = jnp.clip(2.5 * jax.random.uniform(key_of[19], (NH,), jnp.float32) ** steps_of(key_of[19], (NH,), ((0, 16),), -0.2, 0.2), 0.0, 2.5)
    d_skip = jnp.clip(0.5 + 1.0 * jax.random.uniform(key_of[20], (NH,), jnp.float32) ** steps_of(key_of[20], (NH,), ((0, 16),), -0.2, 0.2), 0.5, 1.5)
    weight_ssm_out = scatter_about(key_of[21], (DI, D), DI ** -0.5, 0.125, ((0, 16),))
    weight_attn_out = scatter_about(key_of[22], (QH * HD, D), (QH * HD) ** -0.5, 0.1875, ((0, 16),))
    return {"tokens": tokens, "arrival": arrival, "cache_lengths": cache_lengths, "move_slot": move_slot, "move_target": move_target, "page_table": page_table, "kv_pool": kv_pool, "ssm_state": ssm_state, "conv_x": conv_x, "conv_bc": conv_bc, "norm_gain": norm_gain, "weight_z": weight_z, "weight_x": weight_x, "weight_dt": weight_dt, "weight_bc": weight_bc, "weight_qkv": weight_qkv, "conv_weight_x": conv_weight_x, "conv_weight_bc": conv_weight_bc, "dt_bias": dt_bias, "a_log": a_log, "d_skip": d_skip, "weight_ssm_out": weight_ssm_out, "weight_attn_out": weight_attn_out}


EPSILON = 1e-05
FLOOR_SCORE = -1e+30
PRECISE = lax.Precision.HIGHEST

def residents(move_slot, move_target, row_count, slot_count):
    move_count = move_slot.shape[1]
    devices = jnp.arange(row_count, dtype=jnp.int32)
    matches = move_target[:, None, :] == devices[None, :, None]
    sending = jnp.any(matches, axis=2)
    slot_from = lax.optimization_barrier(jnp.sum(jnp.where(matches, move_slot[:, None, :], 0), axis=2))
    ranking = jnp.cumsum(sending.astype(jnp.int32), axis=0) - 1
    leaving = devices[:, None] * slot_count + slot_from
    turn_order = jnp.arange(move_count, dtype=jnp.int32)
    chosen = sending[:, :, None] & (ranking[:, :, None] == turn_order[None, None, :])
    incoming = lax.optimization_barrier(jnp.sum(jnp.where(chosen, leaving[:, :, None], 0), axis=0))
    places = jnp.arange(slot_count, dtype=jnp.int32)
    vacant = move_slot[:, :, None] == places[None, None, :]
    filled = lax.optimization_barrier(jnp.sum(jnp.where(vacant, incoming[:, :, None], 0), axis=1))
    staying = devices[:, None] * slot_count + places[None, :]
    return jnp.where(jnp.any(vacant, axis=1), filled, staying).astype(jnp.int32)

def reference(tokens, arrival, cache_lengths, move_slot, move_target, page_table, kv_pool, ssm_state, conv_x, conv_bc, norm_gain, weight_z, weight_x, weight_dt, weight_bc, weight_qkv, conv_weight_x, conv_weight_bc, dt_bias, a_log, d_skip, weight_ssm_out, weight_attn_out):
    layout = residents(move_slot, move_target, N_ROWS, SLOTS).reshape(-1)
    inverse = jnp.zeros((REQUESTS,), jnp.int32).at[arrival].set(jnp.arange(REQUESTS, dtype=jnp.int32))
    picked = jnp.take(tokens, inverse[layout], axis=0)
    widened = picked.astype(jnp.float32)
    square_sum = lax.optimization_barrier(jnp.sum(jnp.square(widened), axis=1))
    scaled = (widened * norm_gain.astype(jnp.float32)[None, :]).astype(jnp.bfloat16)
    root_mean = jnp.sqrt(square_sum / D + EPSILON)[:, None]

    def project(weight):
        return (jnp.dot(scaled, weight, preferred_element_type=jnp.float32) / root_mean).astype(jnp.bfloat16)
    gate_in = project(weight_z)
    value_in = project(weight_x)
    step_in = project(weight_dt)
    bc_in = project(weight_bc)
    qkv_in = project(weight_qkv)
    window_x = jnp.concatenate([jnp.take(conv_x, layout, axis=0), value_in[:, None, :]], axis=1)
    window_bc = jnp.concatenate([jnp.take(conv_bc, layout, axis=0), bc_in[:, None, :]], axis=1)
    conv_x_next = window_x[:, 1:]
    conv_bc_next = window_bc[:, 1:]
    value_act = jax.nn.silu(lax.optimization_barrier(jnp.sum(window_x.astype(jnp.float32) * conv_weight_x.astype(jnp.float32)[None], axis=1)))
    bc_act = jax.nn.silu(lax.optimization_barrier(jnp.sum(window_bc.astype(jnp.float32) * conv_weight_bc.astype(jnp.float32)[None], axis=1))).astype(jnp.bfloat16)
    b_in = bc_act[:, :NS].astype(jnp.float32)
    c_out = bc_act[:, NS:].astype(jnp.float32)
    step_size = jax.nn.softplus(step_in.astype(jnp.float32) + dt_bias.astype(jnp.float32)[None, :])
    decay_rate = jnp.exp(-jnp.exp(a_log.astype(jnp.float32))[None, :] * step_size)
    skip_wide = d_skip.astype(jnp.float32)

    def ssm_row(index):
        request = layout[index]
        prior = lax.dynamic_index_in_dim(ssm_state, request, 0, keepdims=False).astype(jnp.float32)
        value_heads = value_act[index].reshape(NH, HP)
        state_new = decay_rate[index][:, None, None] * prior + (step_size[index][:, None] * value_heads)[:, :, None] * b_in[index][None, None, :]
        readout = jnp.einsum('hpn,n->hp', state_new, c_out[index], precision=PRECISE) + skip_wide[:, None] * value_heads
        return (state_new.astype(jnp.bfloat16), readout.reshape(DI))
    ssm_next, readout = lax.map(ssm_row, jnp.arange(REQUESTS, dtype=jnp.int32))
    gated = (readout * jax.nn.silu(gate_in.astype(jnp.float32))).astype(jnp.bfloat16)
    group_size = QH // KVH
    queries = qkv_in[:, :QH * HD].reshape(REQUESTS, KVH, group_size, HD).astype(jnp.float32)
    key_new = qkv_in[:, QH * HD:(QH + KVH) * HD].reshape(REQUESTS, KVH, HD)
    value_new = qkv_in[:, (QH + KVH) * HD:].reshape(REQUESTS, KVH, HD)
    page_total = CTX // PAGE
    logical = jnp.arange(page_total, dtype=jnp.int32)
    page_col = logical % N_COLS
    page_local = logical // N_COLS
    score_scale = HD ** (-0.5)

    def attend(index):
        request = layout[index]
        home_row = request // SLOTS
        home_slot = request % SLOTS
        source_pages = home_row * POOL + page_table[home_row, page_col, home_slot, page_local]
        page_rows = kv_pool[source_pages, page_col].reshape(CTX, 2 * KVH * HD).astype(jnp.float32)
        cached_keys = page_rows[:, :KVH * HD].reshape(CTX, KVH, HD)
        cached_values = page_rows[:, KVH * HD:].reshape(CTX, KVH, HD)
        query_row = queries[index]
        scores = jnp.einsum('kgd,tkd->kgt', query_row, cached_keys, precision=PRECISE) * score_scale
        live_mask = (jnp.arange(CTX) < cache_lengths[request])[None, None, :]
        own_score = jnp.einsum('kgd,kd->kg', query_row, key_new[index].astype(jnp.float32), precision=PRECISE) * score_scale
        row_peak = jnp.maximum(lax.optimization_barrier(jnp.max(jnp.where(live_mask, scores, FLOOR_SCORE), axis=2)), own_score)
        weights = jnp.where(live_mask, jnp.exp(scores - row_peak[:, :, None]), 0.0)
        own_weight = jnp.exp(own_score - row_peak)
        row_total = lax.optimization_barrier(jnp.sum(weights, axis=2)) + own_weight
        weighted = jnp.einsum('kgt,tkd->kgd', weights, cached_values, precision=PRECISE) + own_weight[:, :, None] * value_new[index].astype(jnp.float32)[:, None, :]
        return (weighted / row_total[:, :, None]).reshape(QH * HD).astype(jnp.bfloat16)
    attended = lax.map(attend, jnp.arange(REQUESTS, dtype=jnp.int32))
    mixed = (jnp.dot(gated, weight_ssm_out, preferred_element_type=jnp.float32) + jnp.dot(attended, weight_attn_out, preferred_element_type=jnp.float32)).astype(jnp.bfloat16)
    flat_table = page_table.reshape(N_ROWS, N_COLS, POOL)
    row_ids = jnp.arange(N_ROWS, dtype=jnp.int32)[:, None, None]
    col_ids = jnp.arange(N_COLS, dtype=jnp.int32)[None, :, None]
    owner = jnp.zeros((N_ROWS, N_COLS, POOL), jnp.int32).at[row_ids, col_ids, flat_table].set(jnp.broadcast_to(jnp.arange(POOL, dtype=jnp.int32)[None, None, :], flat_table.shape))
    owner_slot = owner // PPD
    owner_page = owner % PPD
    owner_request = jnp.take(layout, row_ids * SLOTS + owner_slot)
    anchor_row = owner_request // SLOTS
    anchor_slot = owner_request % SLOTS
    source = anchor_row * POOL + page_table[anchor_row, col_ids, anchor_slot, owner_page]
    source = jnp.transpose(source, (0, 2, 1)).reshape(N_ROWS * POOL, N_COLS)
    moved = kv_pool[source, jnp.arange(N_COLS, dtype=jnp.int32)[None, :]]
    served = jnp.arange(REQUESTS, dtype=jnp.int32)
    lengths_now = jnp.take(cache_lengths, layout)
    logical_page = lengths_now // PAGE
    block_col = logical_page % N_COLS
    block_page = logical_page // N_COLS
    offset_in = lengths_now % PAGE
    target_row = served // SLOTS
    target_slot = served % SLOTS
    target_page = target_row * POOL + page_table[target_row, block_col, target_slot, block_page]
    fresh_rows = jnp.concatenate([key_new.reshape(REQUESTS, KVH * HD), value_new.reshape(REQUESTS, KVH * HD)], axis=1)
    kv_next = moved.at[target_page, block_col, offset_in].set(fresh_rows)
    return (mixed, ssm_next, conv_x_next, conv_bc_next, kv_next)
```

```python
import jax
import jax.numpy as jnp
from jax import lax
from jax.experimental import pallas as pl
from jax.experimental.pallas import tpu as pltpu
from jax.sharding import PartitionSpec as P

D = 2048
HP = 64
NS = 256
HD = 128
PAGE = 32
SLOTS = 13
ROWS = 32
COLS = 16
MOVES = 4
EPSILON = 1e-05
FLOOR = -1e30
F32 = jnp.float32
BF16 = jnp.bfloat16
I32 = jnp.int32
MESH = pl.DeviceIdType.MESH


def nt(a, b):
    return lax.dot_general(a, b, (((1,), (1,)), ((), ())), preferred_element_type=F32)


def nn(a, b):
    return jnp.dot(a, b, preferred_element_type=F32)


def silu(v):
    return v / (1.0 + jnp.exp(-v))


def tables_kernel(ms_ref, mt_ref, pt_ref, layout_ref, source_ref, owner_ref):
    row = lax.axis_index("rows")
    for j in range(2 * SLOTS):
        owner_ref[pt_ref[j]] = j
    lane = lax.broadcasted_iota(I32, (128, 128), 1)
    sub = lax.broadcasted_iota(I32, (128, 128), 0)
    eye = lane == sub
    lane_f = lane.astype(F32)
    sub_f = sub.astype(F32)
    ms = jnp.broadcast_to(ms_ref[...].astype(F32), (128, 128))
    mt = jnp.broadcast_to(mt_ref[...].astype(F32), (128, 128))

    def column(v):
        return jnp.sum(jnp.where(eye, v, 0.0), axis=1, keepdims=True)

    def down(v):
        return jnp.sum(v, axis=0, keepdims=True)

    mt_col = column(mt)
    ms_col = column(ms)
    rank = down(jnp.where((mt_col == mt) & (sub < lane), 1.0, 0.0))
    place = 4.0 * mt + jnp.broadcast_to(rank, (128, 128))
    slot_there = down(jnp.where(sub_f == place, jnp.broadcast_to(ms_col, (128, 128)), 0.0))
    place_col = column(place)
    kept_at = (((row - (sub >> 2)) & (ROWS - 1)) * 8 + (sub & 3)).astype(F32)
    source_ref[...] = down(jnp.where(place_col == lane_f, kept_at, 0.0)).astype(I32)
    lane1 = lax.broadcasted_iota(I32, (1, 128), 1)
    goes = 16.0 * mt_ref[...].astype(F32) + slot_there
    left = ((lane1 >> 2) * 16).astype(F32) + ms_ref[...].astype(F32)
    request = ((lane1 >> 2) * SLOTS).astype(F32) + ms_ref[...].astype(F32)
    q = lax.broadcasted_iota(I32, (512, 128), 0)
    q_f = q.astype(F32)
    arrived = jnp.sum(jnp.where(q_f == goes, request, 0.0), axis=1, keepdims=True)
    vacated = jnp.sum(jnp.where(q_f == left, 1.0, 0.0), axis=1, keepdims=True)
    q1 = lax.broadcasted_iota(I32, (512, 1), 0)
    s1 = q1 & 15
    stays = (q1 >> 4) * SLOTS + s1
    layout = jnp.where(vacated > 0.5, arrived.astype(I32), stays)
    layout_ref[...] = jnp.where(s1 < SLOTS, layout, -1)


def mixer_kernel(
    ms, mt, lengths, source, pt, owner, dtb, alog, dskip,
    layout, arrival, tokens, gain, wz, wx, wdt, wbc, wqkv, convp, cwx, cwbc, wssm, wattn,
    pool, state,
    kv_out, state_out, mixed_out, cx_out, cbc_out,
    send1, recv1, send2, recv2, pcomb, scomb, kvn, stn, ccomb, cbuf,
    send_s, recv_s, qbuf, fresh, obuf, pbuf, tbuf, send_a, recv_a, send_o, recv_o,
    s1_sem, r1_sem, s2_sem, r2_sem, ss_sem, rs_sem, sa_sem, ra_sem, so_sem, ro_sem,
    in_sem, out_sem,
):
    row = lax.axis_index("rows")
    col = lax.axis_index("cols")

    pool_copy = pltpu.make_async_copy(pool, pcomb.at[pl.ds(0, 26)], in_sem.at[0])
    state_copy = pltpu.make_async_copy(state, scomb.at[pl.ds(0, SLOTS)], in_sem.at[1])
    pool_copy.start()
    state_copy.start()

    barrier = pltpu.get_barrier_semaphore()

    def greet_rows(d, carry):
        pl.semaphore_signal(barrier, inc=1, device_id=((row + d) & (ROWS - 1), col), device_id_type=MESH)
        return carry

    def greet_cols(d, carry):
        pl.semaphore_signal(barrier, inc=1, device_id=(row, (col + d) & (COLS - 1)), device_id_type=MESH)
        return carry

    lax.fori_loop(1, ROWS, greet_rows, 0)
    lax.fori_loop(1, COLS, greet_cols, 0)

    onehot = jnp.where(layout[...] == arrival[...], 1.0, 0.0).astype(BF16)
    picked = nn(onehot, tokens[...])
    scaled = (picked * gain[...].astype(F32)).astype(BF16)
    squares = jnp.square(picked)
    squares_hi = squares.astype(BF16)
    squares_lo = (squares - squares_hi.astype(F32)).astype(BF16)
    last = (lax.broadcasted_iota(I32, (16, 64), 0) == 15).astype(F32).astype(BF16)
    extra = nt(wdt[...], scaled) + nt(last, squares_hi) + nt(last, squares_lo)
    bc_at = pl.multiple_of(jnp.minimum(col, 3) * 128, 128)
    qkv_at = pl.multiple_of(jnp.maximum(col - 4, 0) * 128, 128)
    shared = jnp.where(
        col < 4, wbc[:, pl.ds(bc_at, 128)].astype(F32), wqkv[:, pl.ds(qkv_at, 128)].astype(F32)
    ).astype(BF16)
    part_z = nn(scaled, wz[...]).reshape(4, 8, 16, 128)
    for u in range(4):
        tile = part_z[u] + extra[:, 128 * u : 128 * (u + 1)][None]
        send1[8 * u : 8 * (u + 1), 5] = tile.astype(BF16)
    send1[:, 6] = nn(scaled, wx[...]).reshape(ROWS, 16, 128).astype(BF16)
    send1[:, 7] = nn(scaled, shared).reshape(ROWS, 16, 128).astype(BF16)

    slots = [ms[MOVES * row + m] for m in range(MOVES)]
    targets = [mt[MOVES * row + m] for m in range(MOVES)]

    def conv_tile(t, carry):
        at = slots[0]
        for m in range(1, MOVES):
            at = jnp.where(targets[m] == t, slots[m], at)
        send1[t, 4] = convp[at]
        return carry

    lax.fori_loop(0, ROWS, conv_tile, 0)
    pool_copy.wait()
    state_copy.wait()

    def cut(m, carry):
        slot = ms[MOVES * row + m]
        for p in range(16):
            r, l = 16 * (p // 2), 128 * (p % 2)
            send1[p, m] = scomb[slot, r : r + 16, l : l + 128]
        for page in range(2):
            g = pt[2 * slot + page]
            for i in range(8):
                r, l = 16 * (i // 4), 128 * (i % 4)
                send1[16 + 8 * page + i, m] = pcomb[g, r : r + 16, l : l + 128]
        return carry

    lax.fori_loop(0, MOVES, cut, 0)

    pl.semaphore_wait(barrier, ROWS + COLS - 2)

    def hop1(d, carry):
        to = (row + d) & (ROWS - 1)
        pltpu.make_async_remote_copy(
            send1.at[to], recv1.at[pl.ds(8 * d, 8)], s1_sem, r1_sem, device_id=(to, col), device_id_type=MESH
        ).start()
        return carry

    lax.fori_loop(1, ROWS, hop1, 0)
    recv1[0:8] = send1[row]
    away1 = recv1.at[pl.ds(8, 8 * (ROWS - 1))]
    pltpu.make_async_copy(away1, away1, r1_sem).wait()

    def pick(t, carry):
        for k in range(MOVES):
            send2[t, k] = recv1[source[MOVES * t + k]]
        return carry

    lax.fori_loop(0, ROWS, pick, 0)

    def hop2(d, carry):
        to = (row + d) & (ROWS - 1)
        pltpu.make_async_remote_copy(
            send2.at[to], recv2.at[d], s2_sem, r2_sem, device_id=(to, col), device_id_type=MESH
        ).start()
        return carry

    lax.fori_loop(1, ROWS, hop2, 0)
    recv2[0] = send2[row]

    def add(d, sums):
        return tuple(sums[j] + recv1[8 * d + 5 + j].astype(F32) for j in range(3))

    zero = jnp.zeros((16, 128), F32)
    sum_z, sum_x, sum_s = lax.fori_loop(0, ROWS, add, (zero, zero, zero))
    lane = lax.broadcasted_iota(I32, (16, 128), 1)
    sub = lax.broadcasted_iota(I32, (16, 128), 0)
    low = lane < HP
    mine = lane == sub + 16 * (row & 7)

    def as_column(k):
        return jnp.sum(jnp.where(mine, jnp.broadcast_to(sum_z[k : k + 1], (16, 128)), 0.0), axis=1, keepdims=True)

    root = jnp.sqrt(as_column(15) / D + EPSILON)
    gate_in = jnp.where(sub < SLOTS, sum_z / root, 0.0).astype(BF16).astype(F32)
    value_in = (sum_x / root).astype(BF16)
    step_in = jnp.where(low, as_column(13) / root, as_column(14) / root).astype(BF16).astype(F32)
    send_s[...] = (sum_s / root).astype(BF16)

    def share(d, carry):
        to = (col + d) & (COLS - 1)
        pltpu.make_async_remote_copy(
            send_s, recv_s.at[d], ss_sem, rs_sem, device_id=(row, to), device_id_type=MESH
        ).start()
        return carry

    lax.fori_loop(1, COLS, share, 0)
    recv_s[0] = send_s[...]

    ccomb[0:SLOTS] = convp[...]
    for k in range(MOVES):
        ccomb[SLOTS + k] = recv1[((source[MOVES * row + k] >> 3) << 3) + 4]
    places = []
    for s in range(SLOTS):
        at = jnp.int32(s)
        for k in range(MOVES):
            at = jnp.where(slots[k] == s, SLOTS + k, at)
        places.append(at)
        cbuf[:, s, :] = ccomb[at].astype(F32)
    for s in range(SLOTS, 16):
        cbuf[:, s, :] = zero

    taps_x = cwx[...].astype(F32)
    taps_bc = cwbc[...].astype(F32)
    conv = value_in.astype(F32) * taps_x[3:4]
    for k in range(3):
        conv = conv + cbuf[k] * taps_x[k : k + 1]
    value_act = silu(conv)
    cx_out[0] = cbuf[1].astype(BF16)
    cx_out[1] = cbuf[2].astype(BF16)
    cx_out[2] = value_in
    head_lanes = lambda ref: jnp.where(low, ref[0], ref[1])
    raw_step = step_in + head_lanes(dtb)
    step = jnp.maximum(raw_step, 0.0) + jnp.log1p(jnp.exp(-jnp.abs(raw_step)))
    decay = jnp.exp(-jnp.exp(head_lanes(alog)) * step)
    grown = step * value_act

    away_s = recv_s.at[pl.ds(1, COLS - 1)]
    pltpu.make_async_copy(away_s, away_s, rs_sem).wait()

    def chunk(c):
        return recv_s[(col - c) & (COLS - 1)]

    act = []
    for c in range(4):
        new = chunk(c)
        lanes = slice(128 * c, 128 * (c + 1))
        conv = new.astype(F32) * taps_bc[3:4, lanes]
        for k in range(3):
            conv = conv + cbuf[3 + 4 * k + c] * taps_bc[k : k + 1, lanes]
        act.append(silu(conv).astype(BF16))
        cbc_out[0, :, lanes] = cbuf[3 + 4 + c].astype(BF16)
        cbc_out[1, :, lanes] = cbuf[3 + 8 + c].astype(BF16)
        cbc_out[2, :, lanes] = new
    b_in = jnp.concatenate(act[:2], axis=1)
    c_out = jnp.concatenate(act[2:], axis=1)
    qbuf[...] = jnp.zeros_like(qbuf)
    for h in range(8):
        lanes = slice(128 * (h // 4), 128 * (h // 4 + 1))
        qbuf[:, h, lanes] = chunk(4 + h).astype(F32)
    for j in range(4):
        fresh[:, 0, 128 * j : 128 * (j + 1)] = chunk(12 + j).astype(F32)

    away2 = recv2.at[pl.ds(1, ROWS - 1)]
    pltpu.make_async_copy(away2, away2, r2_sem).wait()

    def paste(k, carry):
        for p in range(16):
            r, l = 16 * (p // 2), 128 * (p % 2)
            scomb[SLOTS + k, r : r + 16, l : l + 128] = recv2[(row - p) & (ROWS - 1), k]
        for p in range(16):
            i = p % 8
            r, l = 16 * (i // 4), 128 * (i % 4)
            pcomb[26 + 2 * k + p // 8, r : r + 16, l : l + 128] = recv2[(row - 16 - p) & (ROWS - 1), k]
        return carry

    lax.fori_loop(0, MOVES, paste, 0)

    def length_of(s):
        request = row * SLOTS + s
        for k in range(MOVES):
            code = source[MOVES * row + k]
            at = (row - (code >> 3)) & (ROWS - 1)
            request = jnp.where(slots[k] == s, at * SLOTS + ms[MOVES * at + (code & 3)], request)
        return lengths[request]

    line = lax.broadcasted_iota(I32, (PAGE, 512), 0)

    def page(g, carry):
        entry = owner[g]
        s, half = entry >> 1, entry & 1
        at = g
        for k in range(MOVES):
            at = jnp.where(slots[k] == s, 26 + 2 * k + half, at)
        length = length_of(s)
        logical = length >> 5
        here = ((logical & (COLS - 1)) == col) & ((logical >> 4) == half)
        offset = jnp.where(here, length & (PAGE - 1), -1)
        kvn[g] = jnp.where(line == offset, fresh[s].astype(F32), pcomb[at].astype(F32)).astype(BF16)
        return carry

    lax.fori_loop(0, 26, page, 0)
    kv_copy = pltpu.make_async_copy(kvn, kv_out, out_sem.at[0])
    kv_copy.start()

    for ref in (obuf, pbuf, tbuf):
        ref[...] = jnp.zeros_like(ref)
    token = lax.broadcasted_iota(I32, (8, 64), 1)
    position = (token >> 5) * (COLS * PAGE) + col * PAGE + (token & (PAGE - 1))
    head = lax.broadcasted_iota(I32, (8, 128), 0)
    for s in range(SLOTS):
        both = jnp.concatenate([kvn[pt[2 * s]], kvn[pt[2 * s + 1]]], axis=0)
        scores = nt(qbuf[s].astype(BF16), both[:, :256]) * (HD**-0.5)
        live = position <= length_of(s)
        peak = jnp.max(jnp.where(live, scores, FLOOR), axis=1, keepdims=True)
        weights = jnp.where(live, jnp.exp(scores - peak), 0.0)
        summed = nn(weights.astype(BF16), both[:, 256:])
        obuf[:, s, :] = jnp.where(head < 4, summed[:, :128], summed[:, 128:])
        pbuf[:, s, :] = jnp.broadcast_to(peak, (8, 128))
        tbuf[:, s, :] = jnp.broadcast_to(jnp.sum(weights, axis=1, keepdims=True), (8, 128))
    for h in range(8):
        stats = jnp.where(lane == HP, pbuf[h], tbuf[h])
        send_a[2 * h] = jnp.where(low, obuf[h], stats)
        send_a[2 * h + 1] = jnp.where(low, pltpu.roll(obuf[h], HP, 1), stats)

    def attend(d, carry):
        to = (col + d) & (COLS - 1)
        pltpu.make_async_remote_copy(
            send_a.at[to], recv_a.at[d], sa_sem, ra_sem, device_id=(row, to), device_id_type=MESH
        ).start()
        return carry

    lax.fori_loop(1, COLS, attend, 0)
    recv_a[0] = send_a[col]

    read = zero
    for s in range(SLOTS):
        read = jnp.where(sub == s, nt(c_out, scomb[places[s]]), read)
    b_dot_c = jnp.sum(b_in.astype(F32) * c_out.astype(F32), axis=1, keepdims=True)
    readout = decay * read + grown * b_dot_c + head_lanes(dskip) * value_act
    gated = (readout * silu(gate_in)).astype(BF16)
    out_terms = nn(gated, wssm[...])

    away_a = recv_a.at[pl.ds(1, COLS - 1)]
    pltpu.make_async_copy(away_a, away_a, ra_sem).wait()
    top = recv_a[0]
    for d in range(1, COLS):
        top = jnp.maximum(top, recv_a[d])
    top = top[:, HP : HP + 1]
    gathered = zero
    for d in range(COLS):
        part = recv_a[d]
        gathered = gathered + part * jnp.exp(part[:, HP : HP + 1] - top)
    attended = (gathered / gathered[:, HP + 1 : HP + 2]).astype(BF16)
    out_terms = out_terms + nn(attended[:, :HP], wattn[...])
    for c in range(COLS):
        send_o[c] = out_terms[:, 128 * c : 128 * (c + 1)].astype(BF16)

    def project(d, carry):
        to = (col + d) & (COLS - 1)
        pltpu.make_async_remote_copy(
            send_o.at[to], recv_o.at[d], so_sem, ro_sem, device_id=(row, to), device_id_type=MESH
        ).start()
        return carry

    lax.fori_loop(1, COLS, project, 0)
    recv_o[0] = send_o[col]

    columns = jnp.concatenate([grown, decay, jnp.zeros((96, 128), F32)], axis=0).T
    for s in range(SLOTS):
        old = scomb[places[s]].astype(F32)
        new = columns[:, 16 + s : 17 + s] * old + columns[:, s : s + 1] * b_in[s : s + 1].astype(F32)
        stn[s] = new.astype(BF16)
    state_copy_out = pltpu.make_async_copy(stn, state_out, out_sem.at[1])
    state_copy_out.start()

    away_o = recv_o.at[pl.ds(1, COLS - 1)]
    pltpu.make_async_copy(away_o, away_o, ro_sem).wait()
    mixed = zero
    for d in range(COLS):
        mixed = mixed + recv_o[d].astype(F32)
    mixed_out[...] = mixed.astype(BF16)

    sent1 = send1.at[pl.ds(0, ROWS - 1)]
    pltpu.make_async_copy(sent1, sent1, s1_sem).wait()
    sent2 = send2.at[pl.ds(0, ROWS - 1)]
    pltpu.make_async_copy(sent2, sent2, s2_sem).wait()
    for sem, ref in ((ss_sem, recv_s), (sa_sem, send_a), (so_sem, send_o)):
        sent = ref.at[pl.ds(0, COLS - 1)]
        pltpu.make_async_copy(sent, sent, sem).wait()
    kv_copy.wait()
    state_copy_out.wait()


def local(
    tokens, arrival, cache_lengths, move_slot, move_target, page_table, kv_pool, ssm_state, conv_x, conv_bc,
    norm_gain, weight_z, weight_x, weight_dt, weight_bc, weight_qkv, conv_weight_x, conv_weight_bc,
    dt_bias, a_log, d_skip, weight_ssm_out, weight_attn_out,
):
    vmem = pl.BlockSpec(memory_space=pltpu.VMEM)
    smem = pl.BlockSpec(memory_space=pltpu.SMEM)
    anywhere = pl.BlockSpec(memory_space=pl.ANY)
    shape = jax.ShapeDtypeStruct
    pt = page_table.reshape(2 * SLOTS)
    ms = move_slot.reshape(ROWS * MOVES)
    mt = move_target.reshape(ROWS * MOVES)
    layout, source, owner = pl.pallas_call(
        tables_kernel,
        out_shape=(shape((512, 1), I32), shape((1, 128), I32), shape((2 * SLOTS,), I32)),
        in_specs=[vmem, vmem, smem],
        out_specs=(vmem, vmem, smem),
        name="tables",
    )(ms.reshape(1, 128), mt.reshape(1, 128), pt)

    convp = jnp.concatenate(
        [conv_x, conv_bc.reshape(SLOTS, 12, 128), jnp.zeros((SLOTS, 1, 128), BF16)], axis=1
    )
    wdt = jnp.pad(weight_dt.T, ((13, 1), (0, 0)))
    dma = pltpu.SemaphoreType.DMA
    kv_next, state_next, mixed, cx, cbc = pl.pallas_call(
        mixer_kernel,
        out_shape=(
            shape((26, PAGE, 512), BF16),
            shape((SLOTS, 128, NS), BF16),
            shape((16, 128), BF16),
            shape((3, 16, 128), BF16),
            shape((3, 16, 512), BF16),
        ),
        in_specs=[smem] * 9 + [vmem] * 14 + [anywhere] * 2,
        out_specs=(anywhere, anywhere, vmem, vmem, vmem),
        scratch_shapes=[
            pltpu.VMEM((ROWS, 8, 16, 128), BF16),
            pltpu.VMEM((ROWS * 8, 16, 128), BF16),
            pltpu.VMEM((ROWS, MOVES, 16, 128), BF16),
            pltpu.VMEM((ROWS, MOVES, 16, 128), BF16),
            pltpu.VMEM((34, PAGE, 512), BF16),
            pltpu.VMEM((SLOTS + MOVES, 128, NS), BF16),
            pltpu.VMEM((26, PAGE, 512), BF16),
            pltpu.VMEM((SLOTS, 128, NS), BF16),
            pltpu.VMEM((SLOTS + MOVES, 16, 128), BF16),
            pltpu.VMEM((16, 16, 128), F32),
            pltpu.VMEM((16, 128), BF16),
            pltpu.VMEM((COLS, 16, 128), BF16),
            pltpu.VMEM((16, 8, 256), F32),
            pltpu.VMEM((16, 1, 512), F32),
            pltpu.VMEM((8, 16, 128), F32),
            pltpu.VMEM((8, 16, 128), F32),
            pltpu.VMEM((8, 16, 128), F32),
            pltpu.VMEM((COLS, 16, 128), F32),
            pltpu.VMEM((COLS, 16, 128), F32),
            pltpu.VMEM((COLS, 16, 128), BF16),
            pltpu.VMEM((COLS, 16, 128), BF16),
        ]
        + [dma] * 10
        + [dma((2,)), dma((2,))],
        compiler_params=pltpu.CompilerParams(
            collective_id=0, has_side_effects=True, vmem_limit_bytes=48 * 1024 * 1024
        ),
        name="mixer",
    )(
        ms, mt, cache_lengths, source.reshape(128), pt, owner, dt_bias, a_log, d_skip,
        layout, arrival.reshape(1, 416), tokens, norm_gain.reshape(1, 64), weight_z, weight_x, wdt,
        weight_bc, weight_qkv, convp, conv_weight_x, conv_weight_bc, weight_ssm_out, weight_attn_out,
        kv_pool.reshape(26, PAGE, 512), ssm_state.reshape(SLOTS, 128, NS),
    )
    return (
        mixed[:SLOTS],
        state_next.reshape(SLOTS, 2, HP, NS),
        cx.transpose(1, 0, 2)[:SLOTS],
        cbc.transpose(1, 0, 2)[:SLOTS],
        kv_next.reshape(26, 1, PAGE, 512),
    )


def solution(mesh):
    in_specs = (
        P(None, "rows"), P(), P(), P(), P(), P("rows", "cols", None, None), P("rows", "cols", None, None),
        P("rows", "cols", None, None), P("rows", None, "cols"), P("rows", None, None), P("rows"),
        P("rows", "cols"), P("rows", "cols"), P("rows", "cols"), P("rows", None), P("rows", None),
        P(None, "cols"), P(), P("cols"), P("cols"), P("cols"), P("cols", None), P("cols", None),
    )
    out_specs = (
        P("rows", "cols"),
        P("rows", "cols", None, None),
        P("rows", None, "cols"),
        P("rows", None, None),
        P("rows", "cols", None, None),
    )
    return jax.shard_map(local, mesh=mesh, in_specs=in_specs, out_specs=out_specs, check_vma=False)
```

```python
import jax
import jax.numpy as jnp
from jax import lax
from jax.experimental import pallas as pl
from jax.experimental.pallas import tpu as pltpu
from jax.sharding import PartitionSpec as P

D = 2048
HP = 64
NS = 256
HD = 128
PAGE = 32
SLOTS = 13
ROWS = 32
COLS = 16
MOVES = 4
EPSILON = 1e-05
FLOOR = -1e30
F32 = jnp.float32
BF16 = jnp.bfloat16
I32 = jnp.int32
MESH = pl.DeviceIdType.MESH


def nt(a, b):
    return lax.dot_general(a, b, (((1,), (1,)), ((), ())), preferred_element_type=F32)


def nn(a, b):
    return jnp.dot(a, b, preferred_element_type=F32)


def silu(v):
    return v / (1.0 + jnp.exp(-v))


def mixer_kernel(
    ms, mt, lengths, pt, dtb, alog, dskip,
    ms_v, mt_v, arrival, gain, wdt, cwx, cwbc, conv_x, conv_bc,
    tokens, wz, wx, wbc, wqkv, wssm, wattn, pool, state,
    kv_out, state_out, mixed_out, cx_out, cbc_out,
    send1, recv1, send2, recv2, pcomb, scomb, kvn, stn, convp, cbuf, table_v, table,
    send_r, recv_r, send_b, recv_b, send_s, recv_s, qbuf, fresh, obuf, pbuf, tbuf,
    send_a, recv_a, send_o, recv_o, tokens_v, wz_v, wx_v, shared_v, wssm_v, wattn_v,
    s1_sem, r1_sem, s2_sem, r2_sem, sr_sem, rr_sem, sb_sem, rb_sem, ss_sem, rs_sem,
    sa_sem, ra_sem, so_sem, ro_sem, in_sem, table_sem, out_sem,
):
    row = lax.axis_index("rows")
    col = lax.axis_index("cols")
    core = row & 1
    chip = row >> 1
    plane = row >> 3
    member = row & 7

    barrier = pltpu.get_barrier_semaphore()

    def greet_rows(d, carry):
        pl.semaphore_signal(barrier, inc=1, device_id=((row + d) & (ROWS - 1), col), device_id_type=MESH)
        return carry

    def greet_cols(d, carry):
        pl.semaphore_signal(barrier, inc=1, device_id=(row, (col + d) & (COLS - 1)), device_id_type=MESH)
        return carry

    loads = [
        pltpu.make_async_copy(src, dst, in_sem.at[i])
        for i, (src, dst) in enumerate((
            (tokens, tokens_v), (wz, wz_v), (wx, wx_v),
            (pool, pcomb.at[pl.ds(0, 26)]), (state, scomb.at[pl.ds(0, SLOTS)]),
            (wssm, wssm_v), (wattn, wattn_v),
        ))
    ]
    bc_at = pl.multiple_of(jnp.minimum(col, 3) * 128, 128)
    qkv_at = pl.multiple_of(jnp.maximum(col - 4, 0) * 128, 128)
    load_bc = pltpu.make_async_copy(wbc.at[:, pl.ds(bc_at, 128)], shared_v.at[0], in_sem.at[7])
    load_qkv = pltpu.make_async_copy(wqkv.at[:, pl.ds(qkv_at, 128)], shared_v.at[1], in_sem.at[8])
    for load in loads[:3] + [load_bc, load_qkv] + loads[3:]:
        load.start()
    lax.fori_loop(1, ROWS, greet_rows, 0)
    lax.fori_loop(1, COLS, greet_cols, 0)

    lane = lax.broadcasted_iota(I32, (128, 128), 1)
    sub = lax.broadcasted_iota(I32, (128, 128), 0)
    eye = lane == sub
    line_ms = jnp.concatenate([ms_v[m : m + 1, :] for m in range(MOVES)], axis=1)
    line_mt = jnp.concatenate([mt_v[m : m + 1, :] for m in range(MOVES)], axis=1)
    wide = lambda v: jnp.broadcast_to(v, (128, 128))
    across = lambda v: jnp.sum(v, axis=1, keepdims=True)
    down = lambda v: jnp.sum(v, axis=0, keepdims=True)
    mt_col = across(jnp.where(eye, wide(line_mt), 0))
    ms_col = across(jnp.where(eye, wide(line_ms), 0))
    earlier = (sub & (ROWS - 1)) < (lane & (ROWS - 1))
    rank = down(jnp.where((wide(mt_col) == wide(line_mt)) & earlier, 1, 0))
    place = rank * ROWS + line_mt
    slot_there = down(jnp.where(sub == wide(place), wide(ms_col), 0))
    place_col = across(jnp.where(eye, wide(place), 0))
    kept_at = ((row - sub) & (ROWS - 1)) * 8 + (sub >> 5)
    table_v[...] = jnp.zeros_like(table_v)
    table_v[0:1, :] = down(jnp.where(wide(place_col) == lane, kept_at, 0))
    lane1 = lax.broadcasted_iota(I32, (1, 128), 1)
    owners = jnp.zeros((1, 128), I32)
    for s in range(SLOTS):
        for half in range(2):
            owners = jnp.where(lane1 == pt[half, s], 2 * s + half, owners)
    table_v[1:2, :] = owners
    load_table = pltpu.make_async_copy(table_v, table, table_sem)
    load_table.start()
    source_row = lane1 & (ROWS - 1)
    goes = 16 * line_mt + slot_there
    left = 16 * source_row + line_ms
    request = SLOTS * source_row + line_ms
    q = lax.broadcasted_iota(I32, (512, 128), 0)
    arrived = across(jnp.where(q == goes, request, 0))
    vacated = across(jnp.where(q == left, 1, 0))
    q1 = lax.broadcasted_iota(I32, (512, 1), 0)
    layout = jnp.where(vacated > 0, arrived, (q1 >> 4) * SLOTS + (q1 & 15))
    layout = jnp.where((q1 & 15) < SLOTS, layout, -1)

    onehot = jnp.where(layout == arrival[...], 1.0, 0.0).astype(BF16)
    loads[0].wait()
    picked = nt(onehot, tokens_v[...])
    scaled = (picked * gain[...].astype(F32)).astype(BF16)
    squares = jnp.square(picked)
    squares_hi = squares.astype(BF16)
    squares_lo = (squares - squares_hi.astype(F32)).astype(BF16)
    line64 = lax.broadcasted_iota(I32, (16, 64), 0)
    last = jnp.where(line64 == 15, 1.0, 0.0).astype(BF16)
    steps = wdt[...].astype(F32)
    steps = jnp.where(line64 == 13, steps[0:1], jnp.where(line64 == 14, steps[1:2], 0.0)).astype(BF16)
    extra = nt(steps, scaled) + nt(last, squares_hi) + nt(last, squares_lo)
    for load in (loads[1], loads[2], load_bc, load_qkv):
        load.wait()
    part_z = nn(scaled, wz_v[...]).reshape(4, 8, 16, 128)
    part_x = nn(scaled, wx_v[...]).reshape(4, 8, 16, 128).astype(BF16)
    part_s = nn(scaled, shared_v[jnp.where(col < 4, 0, 1)]).reshape(4, 8, 16, 128).astype(BF16)
    for u in range(4):
        send_r[:, 3 * u] = (part_z[u] + extra[:, 128 * u : 128 * (u + 1)][None]).astype(BF16)
        send_r[:, 3 * u + 1] = part_x[u]
        send_r[:, 3 * u + 2] = part_s[u]

    windows = [conv_x[k].astype(F32) for k in range(3)]
    windows += [conv_bc[k, :, 128 * c : 128 * (c + 1)].astype(F32) for k in range(3) for c in range(4)]
    for i, window in enumerate(windows):
        cbuf[0:SLOTS, i, :] = window
    cbuf[:, 15, :] = jnp.zeros((16, 128), F32)
    convp[...] = cbuf[...].astype(BF16)
    slots = [ms[m, row] for m in range(MOVES)]
    targets = [mt[m, row] for m in range(MOVES)]

    def conv_tile(t, carry):
        at = slots[0]
        for m in range(1, MOVES):
            at = jnp.where(targets[m] == t, slots[m], at)
        send1[t, 4] = convp[at]
        return carry

    lax.fori_loop(0, ROWS, conv_tile, 0)
    loads[3].wait()
    loads[4].wait()

    def cut(m, carry):
        slot = ms[m, row]
        for p in range(16):
            r, l = 16 * (p // 2), 128 * (p % 2)
            send1[2 * p + 1, m] = scomb[slot, r : r + 16, l : l + 128]
        for page in range(2):
            g = pt[page, slot]
            for i in range(8):
                r, l = 16 * (i // 4), 128 * (i % 4)
                send1[2 * (8 * page + i), m] = pcomb[g, r : r + 16, l : l + 128]
        return carry

    lax.fori_loop(0, MOVES, cut, 0)

    pl.semaphore_wait(barrier, ROWS + COLS - 2)

    def reduce_in(d, carry):
        to = (member + d) & 7
        pltpu.make_async_remote_copy(
            send_r.at[to], recv_r.at[d], sr_sem, rr_sem, device_id=(plane * 8 + to, col), device_id_type=MESH
        ).start()
        return carry

    lax.fori_loop(1, 8, reduce_in, 0)

    def hop1(kind):
        def send(d, carry):
            to = 2 * ((chip + d) & 15) + kind

            @pl.when(to != row)
            def _():
                pltpu.make_async_remote_copy(
                    send1.at[to], recv1.at[(to - row) & (ROWS - 1)], s1_sem, r1_sem,
                    device_id=(to, col), device_id_type=MESH,
                ).start()

            return carry

        lax.fori_loop(0, 16, send, 0)

    hop1(0)
    hop1(1)
    recv1[0] = send1[row]
    recv_r[0] = send_r[member]
    load_table.wait()

    away_r = recv_r.at[pl.ds(1, 7)]
    pltpu.make_async_copy(away_r, away_r, rr_sem).wait()
    for u in range(4):
        for j in range(3):
            total = recv_r[0, 3 * u + j].astype(F32)
            for d in range(1, 8):
                total = total + recv_r[d, 3 * u + j].astype(F32)
            send_b[u, j] = total.astype(BF16)

    def reduce_across(d, carry):
        to = (plane + d) & 3
        pltpu.make_async_remote_copy(
            send_b.at[to], recv_b.at[d], sb_sem, rb_sem, device_id=(to * 8 + member, col), device_id_type=MESH
        ).start()
        return carry

    lax.fori_loop(1, 4, reduce_across, 0)
    recv_b[0] = send_b[plane]
    away_b = recv_b.at[pl.ds(1, 3)]
    pltpu.make_async_copy(away_b, away_b, rb_sem).wait()

    zero = jnp.zeros((16, 128), F32)
    sum_z, sum_x, sum_s = (
        recv_b[0, j].astype(F32) + recv_b[1, j].astype(F32) + recv_b[2, j].astype(F32) + recv_b[3, j].astype(F32)
        for j in range(3)
    )
    lane = lax.broadcasted_iota(I32, (16, 128), 1)
    sub = lax.broadcasted_iota(I32, (16, 128), 0)
    low = lane < HP
    mine = lane == sub + 16 * member

    def as_column(k):
        return jnp.sum(jnp.where(mine, jnp.broadcast_to(sum_z[k : k + 1], (16, 128)), 0.0), axis=1, keepdims=True)

    root = jnp.sqrt(as_column(15) / D + EPSILON)
    real = sub < SLOTS
    gate_in = jnp.where(real, sum_z / root, 0.0).astype(BF16).astype(F32)
    value_in = jnp.where(real, sum_x / root, 0.0).astype(BF16)
    step_in = jnp.where(low, as_column(13) / root, as_column(14) / root).astype(BF16).astype(F32)
    send_s[...] = jnp.where(real, sum_s / root, 0.0).astype(BF16)

    def share(d, carry):
        to = (col + d) & (COLS - 1)
        pltpu.make_async_remote_copy(
            send_s, recv_s.at[d], ss_sem, rs_sem, device_id=(row, to), device_id_type=MESH
        ).start()
        return carry

    lax.fori_loop(1, COLS, share, 0)
    recv_s[0] = send_s[...]

    away1 = recv1.at[pl.ds(1, ROWS - 1)]
    pltpu.make_async_copy(away1, away1, r1_sem).wait()

    def pick(t, carry):
        for k in range(MOVES):
            code = table[0, ROWS * k + t]
            send2[t, k] = recv1[(code >> 3) & (ROWS - 1), code & 3]
        return carry

    lax.fori_loop(0, ROWS, pick, 0)

    def hop2(d, carry):
        to = (row + d) & (ROWS - 1)
        pltpu.make_async_remote_copy(
            send2.at[to], recv2.at[d], s2_sem, r2_sem.at[core], device_id=(to, col), device_id_type=MESH
        ).start()
        return carry

    lax.fori_loop(1, ROWS, hop2, 0)
    recv2[0] = send2[row]

    def wait_pieces(kind):
        @pl.when(core == kind)
        def _():
            some = recv2.at[pl.ds(0, 15)]
            pltpu.make_async_copy(some, some, r2_sem.at[kind]).wait()

        @pl.when(core != kind)
        def _():
            some = recv2.at[pl.ds(0, 16)]
            pltpu.make_async_copy(some, some, r2_sem.at[kind]).wait()

    codes = [table[0, ROWS * k + row] for k in range(MOVES)]
    places = []
    for s in range(SLOTS):
        at = jnp.int32(s)
        for k in range(MOVES):
            at = jnp.where(slots[k] == s, SLOTS + k, at)
        places.append(at)
    tiles = [recv1[(code >> 3) & (ROWS - 1), 4].astype(F32) for code in codes]
    window = []
    for i in range(15):
        rows_i = jnp.concatenate([windows[i], jnp.zeros((3, 128), F32)], axis=0)
        for k in range(MOVES):
            rows_i = jnp.where(sub == slots[k], jnp.broadcast_to(tiles[k][i : i + 1], (16, 128)), rows_i)
        window.append(rows_i)

    taps_x = cwx[...].astype(F32)
    taps_bc = cwbc[...].astype(F32)
    conv = value_in.astype(F32) * taps_x[3:4]
    for k in range(3):
        conv = conv + window[k] * taps_x[k : k + 1]
    value_act = silu(conv)
    cx_out[0] = window[1][:SLOTS].astype(BF16)
    cx_out[1] = window[2][:SLOTS].astype(BF16)
    cx_out[2] = value_in[:SLOTS]
    head_lanes = lambda ref: jnp.where(low, ref[0], ref[1])
    raw_step = step_in + head_lanes(dtb)
    step = jnp.maximum(raw_step, 0.0) + jnp.log1p(jnp.exp(-jnp.abs(raw_step)))
    decay = jnp.exp(-jnp.exp(head_lanes(alog)) * step)
    grown = step * value_act

    away_s = recv_s.at[pl.ds(1, COLS - 1)]
    pltpu.make_async_copy(away_s, away_s, rs_sem).wait()

    def chunk(c):
        return recv_s[(col - c) & (COLS - 1)]

    act = []
    for c in range(4):
        new = chunk(c)
        lanes = slice(128 * c, 128 * (c + 1))
        conv = new.astype(F32) * taps_bc[3:4, lanes]
        for k in range(3):
            conv = conv + window[3 + 4 * k + c] * taps_bc[k : k + 1, lanes]
        act.append(silu(conv).astype(BF16))
        cbc_out[0, :, lanes] = window[3 + 4 + c][:SLOTS].astype(BF16)
        cbc_out[1, :, lanes] = window[3 + 8 + c][:SLOTS].astype(BF16)
        cbc_out[2, :, lanes] = new[:SLOTS]
    b_in = jnp.concatenate(act[:2], axis=1)
    c_out = jnp.concatenate(act[2:], axis=1)
    qbuf[...] = jnp.zeros_like(qbuf)
    for h in range(8):
        lanes = slice(128 * (h // 4), 128 * (h // 4 + 1))
        qbuf[:, h, lanes] = chunk(4 + h).astype(F32)
    for j in range(4):
        fresh[:, 0, 128 * j : 128 * (j + 1)] = chunk(12 + j).astype(F32)

    wait_pieces(0)

    def paste_pages(k, carry):
        for p in range(16):
            i = p % 8
            r, l = 16 * (i // 4), 128 * (i % 4)
            pcomb[26 + 2 * k + p // 8, r : r + 16, l : l + 128] = recv2[(row - 2 * p) & (ROWS - 1), k]
        return carry

    lax.fori_loop(0, MOVES, paste_pages, 0)

    def length_of(s):
        request = row * SLOTS + s
        for k in range(MOVES):
            at = (row - (codes[k] >> 3)) & (ROWS - 1)
            request = jnp.where(slots[k] == s, at * SLOTS + ms[codes[k] & 3, at], request)
        return lengths[request]

    line = lax.broadcasted_iota(I32, (PAGE, 512), 0)

    def page(g, carry):
        entry = table[1, g]
        s, half = entry >> 1, entry & 1
        at = g
        for k in range(MOVES):
            at = jnp.where(slots[k] == s, 26 + 2 * k + half, at)
        length = length_of(s)
        logical = length >> 5
        here = ((logical & (COLS - 1)) == col) & ((logical >> 4) == half)
        offset = jnp.where(here, length & (PAGE - 1), -1)
        kvn[g] = jnp.where(line == offset, fresh[s].astype(F32), pcomb[at].astype(F32)).astype(BF16)
        return carry

    lax.fori_loop(0, 26, page, 0)
    kv_copy = pltpu.make_async_copy(kvn, kv_out, out_sem.at[0])
    kv_copy.start()

    for ref in (obuf, pbuf, tbuf):
        ref[...] = jnp.zeros_like(ref)
    token = lax.broadcasted_iota(I32, (8, 64), 1)
    position = (token >> 5) * (COLS * PAGE) + col * PAGE + (token & (PAGE - 1))
    head = lax.broadcasted_iota(I32, (8, 128), 0)
    for s in range(SLOTS):
        both = jnp.concatenate([kvn[pt[0, s]], kvn[pt[1, s]]], axis=0)
        scores = nt(qbuf[s].astype(BF16), both[:, :256]) * (HD**-0.5)
        live = position <= length_of(s)
        peak = jnp.max(jnp.where(live, scores, FLOOR), axis=1, keepdims=True)
        weights = jnp.where(live, jnp.exp(scores - peak), 0.0)
        summed = nn(weights.astype(BF16), both[:, 256:])
        obuf[:, s, :] = jnp.where(head < 4, summed[:, :128], summed[:, 128:])
        pbuf[:, s, :] = jnp.broadcast_to(peak, (8, 128))
        tbuf[:, s, :] = jnp.broadcast_to(jnp.sum(weights, axis=1, keepdims=True), (8, 128))
    for h in range(8):
        stats = jnp.where(lane == HP, pbuf[h], tbuf[h])
        send_a[2 * h] = jnp.where(low, obuf[h], stats)
        send_a[2 * h + 1] = jnp.where(low, pltpu.roll(obuf[h], HP, 1), stats)

    def attend(d, carry):
        to = (col + d) & (COLS - 1)
        pltpu.make_async_remote_copy(
            send_a.at[to], recv_a.at[d], sa_sem, ra_sem, device_id=(row, to), device_id_type=MESH
        ).start()
        return carry

    lax.fori_loop(1, COLS, attend, 0)
    recv_a[0] = send_a[col]

    wait_pieces(1)

    def paste_states(k, carry):
        for p in range(16):
            r, l = 16 * (p // 2), 128 * (p % 2)
            scomb[SLOTS + k, r : r + 16, l : l + 128] = recv2[(row - 2 * p - 1) & (ROWS - 1), k]
        return carry

    lax.fori_loop(0, MOVES, paste_states, 0)
    read = zero
    for s in range(SLOTS):
        read = jnp.where(sub == s, nt(c_out, scomb[places[s]]), read)
    b_dot_c = jnp.sum(b_in.astype(F32) * c_out.astype(F32), axis=1, keepdims=True)
    readout = decay * read + grown * b_dot_c + head_lanes(dskip) * value_act
    gated = (readout * silu(gate_in)).astype(BF16)
    loads[5].wait()
    loads[6].wait()
    out_terms = nn(gated, wssm_v[...])

    away_a = recv_a.at[pl.ds(1, COLS - 1)]
    pltpu.make_async_copy(away_a, away_a, ra_sem).wait()
    top = recv_a[0]
    for d in range(1, COLS):
        top = jnp.maximum(top, recv_a[d])
    top = top[:, HP : HP + 1]
    gathered = zero
    for d in range(COLS):
        part = recv_a[d]
        gathered = gathered + part * jnp.exp(part[:, HP : HP + 1] - top)
    attended = (gathered / gathered[:, HP + 1 : HP + 2]).astype(BF16)
    out_terms = out_terms + nn(attended[:, :HP], wattn_v[...])
    for c in range(COLS):
        send_o[c] = out_terms[:, 128 * c : 128 * (c + 1)].astype(BF16)

    def project(d, carry):
        to = (col + d) & (COLS - 1)
        pltpu.make_async_remote_copy(
            send_o.at[to], recv_o.at[d], so_sem, ro_sem, device_id=(row, to), device_id_type=MESH
        ).start()
        return carry

    lax.fori_loop(1, COLS, project, 0)
    recv_o[0] = send_o[col]

    columns = jnp.concatenate([grown, decay, jnp.zeros((96, 128), F32)], axis=0).T
    for s in range(SLOTS):
        old = scomb[places[s]].astype(F32)
        new = columns[:, 16 + s : 17 + s] * old + columns[:, s : s + 1] * b_in[s : s + 1].astype(F32)
        stn[s] = new.astype(BF16)
    state_copy_out = pltpu.make_async_copy(stn, state_out, out_sem.at[1])
    state_copy_out.start()

    away_o = recv_o.at[pl.ds(1, COLS - 1)]
    pltpu.make_async_copy(away_o, away_o, ro_sem).wait()
    mixed = zero
    for d in range(COLS):
        mixed = mixed + recv_o[d].astype(F32)
    mixed_out[...] = mixed[:SLOTS].astype(BF16)

    sent1 = send1.at[pl.ds(0, ROWS - 1)]
    pltpu.make_async_copy(sent1, sent1, s1_sem).wait()
    sent2 = send2.at[pl.ds(0, ROWS - 1)]
    pltpu.make_async_copy(sent2, sent2, s2_sem).wait()
    sent_r = send_r.at[pl.ds(0, 7)]
    pltpu.make_async_copy(sent_r, sent_r, sr_sem).wait()
    sent_b = send_b.at[pl.ds(0, 3)]
    pltpu.make_async_copy(sent_b, sent_b, sb_sem).wait()
    for sem, ref in ((ss_sem, recv_s), (sa_sem, send_a), (so_sem, send_o)):
        sent = ref.at[pl.ds(0, COLS - 1)]
        pltpu.make_async_copy(sent, sent, sem).wait()
    kv_copy.wait()
    state_copy_out.wait()


def emit_kernel(*refs):
    made, out, held, sem = refs[:5], refs[5:10], refs[10:15], refs[15]
    reads = [pltpu.make_async_copy(made[i], held[i], sem.at[i]) for i in range(5)]
    writes = [pltpu.make_async_copy(held[i], out[i], sem.at[5 + i]) for i in range(5)]
    for read in reads:
        read.start()
    for i in (2, 3, 4, 0, 1):
        reads[i].wait()
        writes[i].start()
    for write in writes:
        write.wait()


def local(
    tokens, arrival, cache_lengths, move_slot, move_target, page_table, kv_pool, ssm_state, conv_x, conv_bc,
    norm_gain, weight_z, weight_x, weight_dt, weight_bc, weight_qkv, conv_weight_x, conv_weight_bc,
    dt_bias, a_log, d_skip, weight_ssm_out, weight_attn_out,
):
    vmem = pl.BlockSpec(memory_space=pltpu.VMEM)
    smem = pl.BlockSpec(memory_space=pltpu.SMEM)
    anywhere = pl.BlockSpec(memory_space=pl.ANY)
    ms, mt = move_slot.T, move_target.T
    pt = page_table.reshape(SLOTS, 2).T
    dma = pltpu.SemaphoreType.DMA
    results = (
        jax.ShapeDtypeStruct((26, PAGE, 512), BF16),
        jax.ShapeDtypeStruct((SLOTS, 128, NS), BF16),
        jax.ShapeDtypeStruct((SLOTS, 128), BF16),
        jax.ShapeDtypeStruct((3, SLOTS, 128), BF16),
        jax.ShapeDtypeStruct((3, SLOTS, 512), BF16),
    )
    tile = lambda *lead: pltpu.VMEM((*lead, 16, 128), BF16)
    made = pl.pallas_call(
        mixer_kernel,
        out_shape=results,
        in_specs=[smem] * 7 + [vmem] * 9 + [anywhere] * 9,
        out_specs=(anywhere, anywhere, vmem, vmem, vmem),
        scratch_shapes=[
            tile(ROWS, 5),
            tile(ROWS, 5),
            tile(ROWS, MOVES),
            tile(ROWS, MOVES),
            pltpu.VMEM((34, PAGE, 512), BF16),
            pltpu.VMEM((SLOTS + MOVES, 128, NS), BF16),
            pltpu.VMEM((26, PAGE, 512), BF16),
            pltpu.VMEM((SLOTS, 128, NS), BF16),
            tile(16),
            pltpu.VMEM((16, 16, 128), F32),
            pltpu.VMEM((8, 128), I32),
            pltpu.SMEM((8, 128), I32),
            tile(8, 12),
            tile(8, 12),
            tile(4, 3),
            tile(4, 3),
            tile(),
            tile(COLS),
            pltpu.VMEM((16, 8, 256), F32),
            pltpu.VMEM((16, 1, 512), F32),
            pltpu.VMEM((8, 16, 128), F32),
            pltpu.VMEM((8, 16, 128), F32),
            pltpu.VMEM((8, 16, 128), F32),
            pltpu.VMEM((COLS, 16, 128), F32),
            pltpu.VMEM((COLS, 16, 128), F32),
            tile(COLS),
            tile(COLS),
            pltpu.VMEM((64, 416), BF16),
            pltpu.VMEM((64, 128), BF16),
            pltpu.VMEM((64, 128), BF16),
            pltpu.VMEM((2, 64, 128), BF16),
            pltpu.VMEM((128, D), BF16),
            pltpu.VMEM((64, D), BF16),
        ]
        + [dma] * 3
        + [dma((2,))]
        + [dma] * 10
        + [dma((9,)), dma, dma((2,))],
        compiler_params=pltpu.CompilerParams(
            collective_id=0, has_side_effects=True, vmem_limit_bytes=60 * 1024 * 1024
        ),
        name="mixer",
    )(
        ms, mt, cache_lengths, pt, dt_bias, a_log, d_skip,
        ms, mt, arrival.reshape(1, 416), norm_gain.reshape(1, 64), weight_dt.T, conv_weight_x, conv_weight_bc,
        conv_x.transpose(1, 0, 2), conv_bc.transpose(1, 0, 2),
        tokens.T, weight_z, weight_x, weight_bc, weight_qkv, weight_ssm_out, weight_attn_out,
        kv_pool.reshape(26, PAGE, 512), ssm_state.reshape(SLOTS, 128, NS),
    )
    kv_next, state_next, mixed, cx, cbc = pl.pallas_call(
        emit_kernel,
        out_shape=results,
        in_specs=[anywhere] * 5,
        out_specs=(anywhere,) * 5,
        scratch_shapes=[pltpu.VMEM(r.shape, r.dtype) for r in results] + [dma((10,))],
        name="emit",
    )(*made)
    return (
        mixed,
        state_next.reshape(SLOTS, 2, HP, NS),
        cx.transpose(1, 0, 2),
        cbc.transpose(1, 0, 2),
        kv_next.reshape(26, 1, PAGE, 512),
    )


def solution(mesh):
    in_specs = (
        P(None, "rows"), P(), P(), P(), P(), P("rows", "cols", None, None), P("rows", "cols", None, None),
        P("rows", "cols", None, None), P("rows", None, "cols"), P("rows", None, None), P("rows"),
        P("rows", "cols"), P("rows", "cols"), P("rows", "cols"), P("rows", None), P("rows", None),
        P(None, "cols"), P(), P("cols"), P("cols"), P("cols"), P("cols", None), P("cols", None),
    )
    out_specs = (
        P("rows", "cols"),
        P("rows", "cols", None, None),
        P("rows", None, "cols"),
        P("rows", None, None),
        P("rows", "cols", None, None),
    )
    return jax.shard_map(local, mesh=mesh, in_specs=in_specs, out_specs=out_specs, check_vma=False)
```

```python
import jax
import jax.numpy as jnp
from jax import lax
from jax.experimental import pallas as pl
from jax.experimental.pallas import tpu as pltpu
from jax.sharding import PartitionSpec as P

D = 2048
HP = 64
NS = 256
HD = 128
PAGE = 32
SLOTS = 13
ROWS = 32
COLS = 16
MOVES = 4
EPSILON = 1e-05
FLOOR = -1e30
F32 = jnp.float32
BF16 = jnp.bfloat16
I32 = jnp.int32
MESH = pl.DeviceIdType.MESH


def nt(a, b):
    return lax.dot_general(a, b, (((1,), (1,)), ((), ())), preferred_element_type=F32)


def nn(a, b):
    return jnp.dot(a, b, preferred_element_type=F32)


def silu(v):
    return v / (1.0 + jnp.exp(-v))


def mixer_kernel(
    ms, mt, lengths, pt, dtb, alog, dskip,
    ms_v, mt_v, arrival, gain, wdt, cwx, cwbc, conv_x, conv_bc,
    tokens, wz, wx, wbc, wqkv, wssm, wattn, pool, state,
    kv_out, state_out, mixed_out, cx_out, cbc_out,
    send1, recv1, send2, recv2, pcomb, scomb, kvn, stn, leave, going, passing, came, table_v, table,
    send_r, recv_r, send_b, recv_b, send_s, recv_s, qbuf, fresh,
    send_a, recv_a, send_o, recv_o, tokens_v, wz_v, wx_v, shared_v, wssm_v, wattn_v,
    s1_sem, r1_sem, s2_sem, r2_sem, sr_sem, rr_sem, sb_sem, rb_sem, ss_sem, rs_sem,
    sa_sem, ra_sem, so_sem, ro_sem, in_sem, table_sem, out_sem,
):
    row = lax.axis_index("rows")
    col = lax.axis_index("cols")
    core = row & 1
    chip = row >> 1
    plane = row >> 3
    member = row & 7

    barrier = pltpu.get_barrier_semaphore()

    def greet_rows(d, carry):
        pl.semaphore_signal(barrier, inc=1, device_id=((row + d) & (ROWS - 1), col), device_id_type=MESH)
        return carry

    def greet_cols(d, carry):
        pl.semaphore_signal(barrier, inc=1, device_id=(row, (col + d) & (COLS - 1)), device_id_type=MESH)
        return carry

    loads = [
        pltpu.make_async_copy(src, dst, in_sem.at[i])
        for i, (src, dst) in enumerate((
            (tokens, tokens_v), (wz, wz_v), (wx, wx_v),
            (pool, pcomb.at[pl.ds(0, 26)]), (state, scomb.at[pl.ds(0, SLOTS)]),
            (wssm, wssm_v), (wattn, wattn_v),
        ))
    ]
    bc_at = pl.multiple_of(jnp.minimum(col, 3) * 128, 128)
    qkv_at = pl.multiple_of(jnp.maximum(col - 4, 0) * 128, 128)
    load_bc = pltpu.make_async_copy(wbc.at[:, pl.ds(bc_at, 128)], shared_v.at[0], in_sem.at[7])
    load_qkv = pltpu.make_async_copy(wqkv.at[:, pl.ds(qkv_at, 128)], shared_v.at[1], in_sem.at[8])
    for load in loads[3:5] + loads[:3] + [load_bc, load_qkv] + loads[5:]:
        load.start()
    lax.fori_loop(1, ROWS, greet_rows, 0)
    lax.fori_loop(1, COLS, greet_cols, 0)

    slots = [ms[m, row] for m in range(MOVES)]
    targets = [mt[m, row] for m in range(MOVES)]

    def cut_pages(m, carry):
        slot = ms[m, row]
        for page in range(2):
            g = pt[page, slot]
            for i in range(8):
                r, l = 16 * (i // 4), 128 * (i % 4)
                send1[2 * (8 * page + i), m] = pcomb[g, r : r + 16, l : l + 128]
        return carry

    loads[3].wait()
    lax.fori_loop(0, MOVES, cut_pages, 0)

    pl.semaphore_wait(barrier, ROWS + COLS - 2)

    def hop1(kind):
        def send(d, carry):
            to = 2 * ((chip + d) & 15) + kind

            @pl.when(to != row)
            def _():
                pltpu.make_async_remote_copy(
                    send1.at[to], recv1.at[(to - row) & (ROWS - 1)], s1_sem, r1_sem,
                    device_id=(to, col), device_id_type=MESH,
                ).start()

            return carry

        lax.fori_loop(0, 16, send, 0)

    hop1(0)

    def cut_states(m, carry):
        slot = ms[m, row]
        for p in range(16):
            r, l = 16 * (p // 2), 128 * (p % 2)
            send1[2 * p + 1, m] = scomb[slot, r : r + 16, l : l + 128]
        return carry

    loads[4].wait()
    lax.fori_loop(0, MOVES, cut_states, 0)

    @pl.when(core == 1)
    def _():
        hop1(1)

    lane = lax.broadcasted_iota(I32, (128, 128), 1)
    sub = lax.broadcasted_iota(I32, (128, 128), 0)
    eye = lane == sub
    line_ms = jnp.concatenate([ms_v[m : m + 1, :] for m in range(MOVES)], axis=1)
    line_mt = jnp.concatenate([mt_v[m : m + 1, :] for m in range(MOVES)], axis=1)
    wide = lambda v: jnp.broadcast_to(v, (128, 128))
    across = lambda v: jnp.sum(v, axis=1, keepdims=True)
    down = lambda v: jnp.sum(v, axis=0, keepdims=True)
    mt_col = across(jnp.where(eye, wide(line_mt), 0))
    ms_col = across(jnp.where(eye, wide(line_ms), 0))
    earlier = (sub & (ROWS - 1)) < (lane & (ROWS - 1))
    rank = down(jnp.where((wide(mt_col) == wide(line_mt)) & earlier, 1, 0))
    place = rank * ROWS + line_mt
    slot_there = down(jnp.where(sub == wide(place), wide(ms_col), 0))
    place_col = across(jnp.where(eye, wide(place), 0))
    kept_at = ((row - sub) & (ROWS - 1)) * 8 + (sub >> 5)
    table_v[...] = jnp.zeros_like(table_v)
    table_v[0:1, :] = down(jnp.where(wide(place_col) == lane, kept_at, 0))
    lane1 = lax.broadcasted_iota(I32, (1, 128), 1)
    owners = jnp.zeros((1, 128), I32)
    for s in range(SLOTS):
        for half in range(2):
            owners = jnp.where(lane1 == pt[half, s], 2 * s + half, owners)
    table_v[1:2, :] = owners
    load_table = pltpu.make_async_copy(table_v, table, table_sem)
    load_table.start()
    source_row = lane1 & (ROWS - 1)
    goes = 16 * line_mt + slot_there
    left = 16 * source_row + line_ms
    request = SLOTS * source_row + line_ms
    q = lax.broadcasted_iota(I32, (512, 128), 0)
    arrived = across(jnp.where(q == goes, request, 0))
    vacated = across(jnp.where(q == left, 1, 0))
    q1 = lax.broadcasted_iota(I32, (512, 1), 0)
    layout = jnp.where(vacated > 0, arrived, (q1 >> 4) * SLOTS + (q1 & 15))
    layout = jnp.where((q1 & 15) < SLOTS, layout, -1)

    onehot = jnp.where(layout == arrival[...], 1.0, 0.0).astype(BF16)
    loads[0].wait()
    picked = nt(onehot, tokens_v[...])
    scaled = (picked * gain[...].astype(F32)).astype(BF16)
    squares = jnp.square(picked)
    squares_hi = squares.astype(BF16)
    squares_lo = (squares - squares_hi.astype(F32)).astype(BF16)
    line64 = lax.broadcasted_iota(I32, (16, 64), 0)
    last = jnp.where(line64 == 15, 1.0, 0.0).astype(BF16)
    steps = wdt[...].astype(F32)
    steps = jnp.where(line64 == 13, steps[0:1], jnp.where(line64 == 14, steps[1:2], 0.0)).astype(BF16)
    extra = nt(steps, scaled) + nt(last, squares_hi) + nt(last, squares_lo)
    for load in (loads[1], loads[2], load_bc, load_qkv):
        load.wait()
    part_z = nn(scaled, wz_v[...]).reshape(4, 8, 16, 128)
    part_x = nn(scaled, wx_v[...]).reshape(4, 8, 16, 128).astype(BF16)
    part_s = nn(scaled, shared_v[jnp.where(col < 4, 0, 1)]).reshape(4, 8, 16, 128).astype(BF16)
    windows = [conv_x[k].astype(F32) for k in range(3)]
    windows += [conv_bc[k, :, 128 * c : 128 * (c + 1)].astype(F32) for k in range(3) for c in range(4)]
    lane16 = lax.broadcasted_iota(I32, (16, 128), 1)
    quarter = lane16 >> 5
    pad = jnp.zeros((3, 128), F32)
    bc_lanes = pl.ds(pl.multiple_of((col >> 2) * 128, 128), 128)
    taps = jnp.zeros((16, 128), F32)
    for k in range(3):
        tap = jnp.concatenate([conv_bc[k, :, bc_lanes].astype(F32), pad], axis=0)
        taps = jnp.where(quarter == k, pltpu.roll(tap, (32 * (k - (col & 3))) & 127, 1), taps)
        leave[:, k, :] = jnp.concatenate([windows[k], pad], axis=0)
    leave[:, 3, :] = taps

    def conv_rows(m, carry):
        for u in range(4):
            at = slots[0]
            for k in range(1, MOVES):
                at = jnp.where(targets[k] == 8 * u + m, slots[k], at)
            going[m, 4 * u : 4 * u + 4, :] = leave[at][0:4]
        return carry

    lax.fori_loop(0, 8, conv_rows, 0)
    send_r[:, 12] = going[...].astype(BF16)
    for u in range(4):
        send_r[:, 3 * u] = (part_z[u] + extra[:, 128 * u : 128 * (u + 1)][None]).astype(BF16)
        send_r[:, 3 * u + 1] = part_x[u]
        send_r[:, 3 * u + 2] = part_s[u]

    def reduce_in(d, carry):
        to = (member + d) & 7
        pltpu.make_async_remote_copy(
            send_r.at[to], recv_r.at[d], sr_sem, rr_sem, device_id=(plane * 8 + to, col), device_id_type=MESH
        ).start()
        return carry

    lax.fori_loop(1, 8, reduce_in, 0)

    recv_r[0] = send_r[member]

    load_table.wait()

    away_r = recv_r.at[pl.ds(1, 7)]
    pltpu.make_async_copy(away_r, away_r, rr_sem).wait()
    for u in range(4):
        for j in range(3):
            total = recv_r[0, 3 * u + j].astype(F32)
            for d in range(1, 8):
                total = total + recv_r[d, 3 * u + j].astype(F32)
            send_b[u, j] = total.astype(BF16)
    for d in range(8):
        rows_d = recv_r[d, 12].astype(F32)
        for u in range(4):
            passing[u, 4 * d : 4 * d + 4, :] = rows_d[4 * u : 4 * u + 4]
    for u in range(4):
        send_b[u, 3] = passing[u, 0:16].astype(BF16)
        send_b[u, 4] = passing[u, 16:32].astype(BF16)

    def reduce_across(d, carry):
        to = (plane + d) & 3
        pltpu.make_async_remote_copy(
            send_b.at[to], recv_b.at[d], sb_sem, rb_sem, device_id=(to * 8 + member, col), device_id_type=MESH
        ).start()
        return carry

    lax.fori_loop(1, 4, reduce_across, 0)

    away1 = recv1.at[pl.ds(1, ROWS - 1)]

    def pick(t, carry):
        for k in range(MOVES):
            code = table[0, ROWS * k + t]
            send2[t, k] = recv1[(code >> 3) & (ROWS - 1), code & 3]
        return carry

    def hop2(d, carry):
        to = (row + d) & (ROWS - 1)
        pltpu.make_async_remote_copy(
            send2.at[to], recv2.at[d], s2_sem, r2_sem.at[core], device_id=(to, col), device_id_type=MESH
        ).start()
        return carry

    def second_hop(kind):
        @pl.when(core == kind)
        def _():
            recv1[0] = send1[row]
            pltpu.make_async_copy(away1, away1, r1_sem).wait()
            lax.fori_loop(0, ROWS, pick, 0)
            lax.fori_loop(1, ROWS, hop2, 0)
            recv2[0] = send2[row]

    second_hop(0)

    @pl.when(core == 0)
    def _():
        hop1(1)

    recv_b[0] = send_b[plane]
    away_b = recv_b.at[pl.ds(1, 3)]
    pltpu.make_async_copy(away_b, away_b, rb_sem).wait()

    zero = jnp.zeros((16, 128), F32)
    sum_z, sum_x, sum_s = (
        recv_b[0, j].astype(F32) + recv_b[1, j].astype(F32) + recv_b[2, j].astype(F32) + recv_b[3, j].astype(F32)
        for j in range(3)
    )
    lane = lax.broadcasted_iota(I32, (16, 128), 1)
    sub = lax.broadcasted_iota(I32, (16, 128), 0)
    low = lane < HP
    mine = lane == sub + 16 * member

    def as_column(k):
        return jnp.sum(jnp.where(mine, jnp.broadcast_to(sum_z[k : k + 1], (16, 128)), 0.0), axis=1, keepdims=True)

    root = jnp.sqrt(as_column(15) / D + EPSILON)
    real = sub < SLOTS
    gate_in = jnp.where(real, sum_z / root, 0.0).astype(BF16).astype(F32)
    value_in = jnp.where(real, sum_x / root, 0.0).astype(BF16)
    step_in = jnp.where(low, as_column(13) / root, as_column(14) / root).astype(BF16).astype(F32)

    for e in range(4):
        for half in range(2):
            rows_e = recv_b[e, 3 + half].astype(F32)
            for d in range(4):
                came[8 * e + 4 * half + d, 0:4, :] = rows_e[4 * d : 4 * d + 4]
    codes = [table[0, ROWS * k + row] for k in range(MOVES)]
    tiles = []
    for code in codes:
        at = (row - (code >> 3)) & (ROWS - 1)
        tiles.append(came[8 * ((plane - (at >> 3)) & 3) + ((member - (at & 7)) & 7)])
    quarter = lane >> 5
    bc_rows = zero
    for k in range(3):
        for m in range(MOVES):
            moved = jnp.broadcast_to(tiles[m][3:4], (16, 128))
            moved = moved if m == k else pltpu.roll(moved, (32 * (m - k)) % 128, 1)
            bc_rows = jnp.where((sub == SLOTS + k) & (quarter == m), moved, bc_rows)
    send_s[...] = jnp.where(real, sum_s / root, bc_rows).astype(BF16)

    def share(d, carry):
        to = (col + d) & (COLS - 1)
        pltpu.make_async_remote_copy(
            send_s, recv_s.at[d], ss_sem, rs_sem, device_id=(row, to), device_id_type=MESH
        ).start()
        return carry

    lax.fori_loop(1, COLS, share, 0)
    recv_s[0] = send_s[...]

    second_hop(1)

    def wait_pieces(kind):
        @pl.when(core == kind)
        def _():
            some = recv2.at[pl.ds(0, 15)]
            pltpu.make_async_copy(some, some, r2_sem.at[kind]).wait()

        @pl.when(core != kind)
        def _():
            some = recv2.at[pl.ds(0, 16)]
            pltpu.make_async_copy(some, some, r2_sem.at[kind]).wait()

    def with_arrived(i, rows_of):
        rows_i = jnp.concatenate([windows[i], jnp.zeros((3, 128), F32)], axis=0)
        for k in range(MOVES):
            rows_i = jnp.where(sub == slots[k], jnp.broadcast_to(rows_of(k), (16, 128)), rows_i)
        return rows_i

    window = [with_arrived(i, lambda k, i=i: tiles[k][i : i + 1]) for i in range(3)]

    taps_x = cwx[...].astype(F32)
    taps_bc = cwbc[...].astype(F32)
    conv = value_in.astype(F32) * taps_x[3:4]
    for k in range(3):
        conv = conv + window[k] * taps_x[k : k + 1]
    value_act = silu(conv)
    cx_out[0] = window[1][:SLOTS].astype(BF16)
    cx_out[1] = window[2][:SLOTS].astype(BF16)
    cx_out[2] = value_in[:SLOTS]
    head_lanes = lambda ref: jnp.where(low, ref[0], ref[1])
    raw_step = step_in + head_lanes(dtb)
    step = jnp.maximum(raw_step, 0.0) + jnp.log1p(jnp.exp(-jnp.abs(raw_step)))
    decay = jnp.exp(-jnp.exp(head_lanes(alog)) * step)
    grown = step * value_act

    away_s = recv_s.at[pl.ds(1, COLS - 1)]
    pltpu.make_async_copy(away_s, away_s, rs_sem).wait()

    def chunk(c):
        return recv_s[(col - c) & (COLS - 1)]

    for c in range(4):
        joined = []
        for m in range(MOVES):
            rows_m = zero
            for j in range(4):
                other = chunk(4 * c + j).astype(F32)
                other = other if j == m else pltpu.roll(other, (32 * (j - m)) % 128, 1)
                rows_m = jnp.where(quarter == j, other, rows_m)
            joined.append(rows_m)
        window += [
            with_arrived(3 + 4 * k + c, lambda m, k=k: joined[m][SLOTS + k : SLOTS + k + 1]) for k in range(3)
        ]
    act = []
    for c in range(4):
        new = chunk(c)
        lanes = slice(128 * c, 128 * (c + 1))
        conv = new.astype(F32) * taps_bc[3:4, lanes]
        for k in range(3):
            conv = conv + window[3 + 3 * c + k] * taps_bc[k : k + 1, lanes]
        act.append(silu(conv).astype(BF16))
        cbc_out[0, :, lanes] = window[3 + 3 * c + 1][:SLOTS].astype(BF16)
        cbc_out[1, :, lanes] = window[3 + 3 * c + 2][:SLOTS].astype(BF16)
        cbc_out[2, :, lanes] = new[:SLOTS]
    b_in = jnp.concatenate(act[:2], axis=1)
    c_out = jnp.concatenate(act[2:], axis=1)

    qbuf[...] = jnp.zeros_like(qbuf)
    for h in range(8):
        lanes = slice(128 * (h // 4), 128 * (h // 4 + 1))
        qbuf[:, h, lanes] = chunk(4 + h).astype(F32)
    for j in range(4):
        fresh[:, 0, 128 * j : 128 * (j + 1)] = chunk(12 + j).astype(F32)

    def length_of(s):
        request = row * SLOTS + s
        for k in range(MOVES):
            at = (row - (codes[k] >> 3)) & (ROWS - 1)
            request = jnp.where(slots[k] == s, at * SLOTS + ms[codes[k] & 3, at], request)
        return lengths[request]

    line = lax.broadcasted_iota(I32, (PAGE, 512), 0)

    def page(at, s, half):
        length = length_of(s)
        logical = length >> 5
        here = ((logical & (COLS - 1)) == col) & ((logical >> 4) == half)
        offset = jnp.where(here, length & (PAGE - 1), -1)
        return jnp.where(line == offset, fresh[s].astype(F32), pcomb[at].astype(F32)).astype(BF16)

    def own_page(g, carry):
        entry = table[1, g]
        kvn[g] = page(g, entry >> 1, entry & 1)
        return carry

    lax.fori_loop(0, 26, own_page, 0)
    kv_copy = pltpu.make_async_copy(kvn.at[pl.ds(0, 26)], kv_out.at[pl.ds(0, 26)], out_sem.at[0])
    kv_copy.start()

    token = lax.broadcasted_iota(I32, (8, 64), 1)
    position = (token >> 5) * (COLS * PAGE) + col * PAGE + (token & (PAGE - 1))
    head = lax.broadcasted_iota(I32, (8, 128), 0)
    lane8 = lax.broadcasted_iota(I32, (8, 128), 1)

    def attention(s, first, second):
        both = jnp.concatenate([first, second], axis=0)
        scores = nt(qbuf[s].astype(BF16), both[:, :256]) * (HD**-0.5)
        live = position <= length_of(s)
        peak = jnp.max(jnp.where(live, scores, FLOOR), axis=1, keepdims=True)
        weights = jnp.where(live, jnp.exp(scores - peak), 0.0)
        summed = nn(weights.astype(BF16), both[:, 256:])
        summed = jnp.where(head < 4, summed[:, :128], summed[:, 128:])
        stats = jnp.where(lane8 == HP, peak, jnp.sum(weights, axis=1, keepdims=True))
        return jnp.where(lane8 < HP, summed, stats), jnp.where(lane8 < HP, pltpu.roll(summed, HP, 1), stats)

    for s in range(SLOTS):
        send_a[:, 0, s, :], send_a[:, 1, s, :] = attention(s, kvn[pt[0, s]], kvn[pt[1, s]])
    for s in range(SLOTS, 16):
        send_a[:, 0, s, :] = jnp.zeros((8, 128), F32)
        send_a[:, 1, s, :] = jnp.zeros((8, 128), F32)

    wait_pieces(0)

    def paste_pages(k, carry):
        for p in range(16):
            i = p % 8
            r, l = 16 * (i // 4), 128 * (i % 4)
            pcomb[26 + 2 * k + p // 8, r : r + 16, l : l + 128] = recv2[(row - 2 * p) & (ROWS - 1), k]
        for half in range(2):
            kvn[26 + 2 * k + half] = page(26 + 2 * k + half, ms[k, row], half)
        return carry

    lax.fori_loop(0, MOVES, paste_pages, 0)
    kv_copy2 = pltpu.make_async_copy(kvn.at[pl.ds(26, 8)], kv_out.at[pl.ds(26, 8)], out_sem.at[1])
    kv_copy2.start()
    found = [attention(slots[k], kvn[26 + 2 * k], kvn[27 + 2 * k]) for k in range(MOVES)]
    for h in range(8):
        for half in range(2):
            tile = send_a[h, half]
            for k in range(MOVES):
                tile = jnp.where(sub == slots[k], jnp.broadcast_to(found[k][half][h : h + 1], (16, 128)), tile)
            send_a[h, half] = tile

    def attend(d, carry):
        to = (col + d) & (COLS - 1)
        pltpu.make_async_remote_copy(
            send_a.at[to >> 1, to & 1], recv_a.at[d], sa_sem, ra_sem, device_id=(row, to), device_id_type=MESH
        ).start()
        return carry

    lax.fori_loop(1, COLS, attend, 0)
    recv_a[0] = send_a[col >> 1, col & 1]

    read = zero
    for s in range(SLOTS):
        read = jnp.where(sub == s, nt(c_out, scomb[s]), read)
    columns = jnp.concatenate([grown, decay, jnp.zeros((96, 128), F32)], axis=0).T
    for s in range(SLOTS):
        old = scomb[s].astype(F32)
        new = columns[:, 16 + s : 17 + s] * old + columns[:, s : s + 1] * b_in[s : s + 1].astype(F32)
        stn[s] = new.astype(BF16)
    own_states = pl.ds(0, SLOTS)
    state_copy_out = pltpu.make_async_copy(stn.at[own_states], state_out.at[own_states], out_sem.at[2])
    state_copy_out.start()
    b_dot_c = jnp.sum(b_in.astype(F32) * c_out.astype(F32), axis=1, keepdims=True)
    loads[5].wait()
    loads[6].wait()

    wait_pieces(1)

    def paste_states(k, carry):
        for p in range(16):
            r, l = 16 * (p // 2), 128 * (p % 2)
            scomb[SLOTS + k, r : r + 16, l : l + 128] = recv2[(row - 2 * p - 1) & (ROWS - 1), k]
        return carry

    lax.fori_loop(0, MOVES, paste_states, 0)
    for k in range(MOVES):
        read = jnp.where(sub == slots[k], nt(c_out, scomb[SLOTS + k]), read)
    readout = decay * read + grown * b_dot_c + head_lanes(dskip) * value_act
    gated = (readout * silu(gate_in)).astype(BF16)
    out_terms = nn(gated, wssm_v[...])

    away_a = recv_a.at[pl.ds(1, COLS - 1)]
    pltpu.make_async_copy(away_a, away_a, ra_sem).wait()
    top = recv_a[0]
    for d in range(1, COLS):
        top = jnp.maximum(top, recv_a[d])
    top = top[:, HP : HP + 1]
    gathered = zero
    for d in range(COLS):
        part = recv_a[d]
        gathered = gathered + part * jnp.exp(part[:, HP : HP + 1] - top)
    attended = jnp.where(real, gathered / gathered[:, HP + 1 : HP + 2], 0.0).astype(BF16)
    out_terms = out_terms + nn(attended[:, :HP], wattn_v[...])
    for c in range(COLS):
        send_o[c] = out_terms[:, 128 * c : 128 * (c + 1)].astype(BF16)

    def project(d, carry):
        to = (col + d) & (COLS - 1)
        pltpu.make_async_remote_copy(
            send_o.at[to], recv_o.at[d], so_sem, ro_sem, device_id=(row, to), device_id_type=MESH
        ).start()
        return carry

    lax.fori_loop(1, COLS, project, 0)
    recv_o[0] = send_o[col]

    lanes = lax.broadcasted_iota(I32, (128, 128), 1)
    rows_b = lax.broadcasted_iota(I32, (16, 256), 0)
    for k in range(MOVES):
        up = jnp.sum(jnp.where(lanes == slots[k], columns, 0.0), axis=1, keepdims=True)
        down_by = jnp.sum(jnp.where(lanes == slots[k] + 16, columns, 0.0), axis=1, keepdims=True)
        b_row = jnp.sum(jnp.where(rows_b == slots[k], b_in.astype(F32), 0.0), axis=0, keepdims=True)
        stn[SLOTS + k] = (down_by * scomb[SLOTS + k].astype(F32) + up * b_row).astype(BF16)
    new_states = pl.ds(SLOTS, MOVES)
    state_copy2 = pltpu.make_async_copy(stn.at[new_states], state_out.at[new_states], out_sem.at[3])
    state_copy2.start()

    away_o = recv_o.at[pl.ds(1, COLS - 1)]
    pltpu.make_async_copy(away_o, away_o, ro_sem).wait()
    mixed = zero
    for d in range(COLS):
        mixed = mixed + recv_o[d].astype(F32)
    mixed_out[...] = mixed[:SLOTS].astype(BF16)

    sent1 = send1.at[pl.ds(0, ROWS - 1)]
    pltpu.make_async_copy(sent1, sent1, s1_sem).wait()
    sent2 = send2.at[pl.ds(0, ROWS - 1)]
    pltpu.make_async_copy(sent2, sent2, s2_sem).wait()
    sent_r = send_r.at[pl.ds(0, 7)]
    pltpu.make_async_copy(sent_r, sent_r, sr_sem).wait()
    sent_b = send_b.at[pl.ds(0, 3)]
    pltpu.make_async_copy(sent_b, sent_b, sb_sem).wait()
    for sem, ref in ((ss_sem, recv_s), (sa_sem, recv_a), (so_sem, send_o)):
        sent = ref.at[pl.ds(0, COLS - 1)]
        pltpu.make_async_copy(sent, sent, sem).wait()
    for copy in (kv_copy, kv_copy2, state_copy_out, state_copy2):
        copy.wait()


def emit_kernel(ms, pt, *refs):
    made, out, held, sem = refs[:5], refs[5:10], refs[10:15], refs[15]
    row = lax.axis_index("rows")
    ready = list(held)
    ready[0] = held[0].at[pl.ds(0, 26)]
    ready[1] = held[1].at[pl.ds(0, SLOTS)]
    reads = [pltpu.make_async_copy(made[i], held[i], sem.at[i]) for i in range(5)]
    writes = [pltpu.make_async_copy(ready[i], out[i], sem.at[5 + i]) for i in range(5)]
    for read in reads:
        read.start()
    for i in (2, 3, 4, 0, 1):
        reads[i].wait()
        for k in range(MOVES):
            slot = ms[k, row]
            if i == 0:
                held[0][pt[0, slot]] = held[0][26 + 2 * k]
                held[0][pt[1, slot]] = held[0][27 + 2 * k]
            if i == 1:
                held[1][slot] = held[1][SLOTS + k]
        writes[i].start()
    for write in writes:
        write.wait()


def local(
    tokens, arrival, cache_lengths, move_slot, move_target, page_table, kv_pool, ssm_state, conv_x, conv_bc,
    norm_gain, weight_z, weight_x, weight_dt, weight_bc, weight_qkv, conv_weight_x, conv_weight_bc,
    dt_bias, a_log, d_skip, weight_ssm_out, weight_attn_out,
):
    vmem = pl.BlockSpec(memory_space=pltpu.VMEM)
    smem = pl.BlockSpec(memory_space=pltpu.SMEM)
    anywhere = pl.BlockSpec(memory_space=pl.ANY)
    ms, mt = move_slot.T, move_target.T
    pt = page_table.reshape(SLOTS, 2).T
    dma = pltpu.SemaphoreType.DMA
    results = (
        jax.ShapeDtypeStruct((26, PAGE, 512), BF16),
        jax.ShapeDtypeStruct((SLOTS, 128, NS), BF16),
        jax.ShapeDtypeStruct((SLOTS, 128), BF16),
        jax.ShapeDtypeStruct((3, SLOTS, 128), BF16),
        jax.ShapeDtypeStruct((3, SLOTS, 512), BF16),
    )
    tile = lambda *lead: pltpu.VMEM((*lead, 16, 128), BF16)
    made = pl.pallas_call(
        mixer_kernel,
        out_shape=(
            jax.ShapeDtypeStruct((34, PAGE, 512), BF16),
            jax.ShapeDtypeStruct((SLOTS + MOVES, 128, NS), BF16),
            *results[2:],
        ),
        in_specs=[smem] * 7 + [vmem] * 9 + [anywhere] * 9,
        out_specs=(anywhere, anywhere, vmem, vmem, vmem),
        scratch_shapes=[
            tile(ROWS, MOVES),
            tile(ROWS, MOVES),
            tile(ROWS, MOVES),
            tile(ROWS, MOVES),
            pltpu.VMEM((34, PAGE, 512), BF16),
            pltpu.VMEM((SLOTS + MOVES, 128, NS), BF16),
            pltpu.VMEM((34, PAGE, 512), BF16),
            pltpu.VMEM((SLOTS + MOVES, 128, NS), BF16),
            pltpu.VMEM((16, 8, 128), F32),
            pltpu.VMEM((8, 16, 128), F32),
            pltpu.VMEM((4, 32, 128), F32),
            pltpu.VMEM((ROWS, 8, 128), F32),
            pltpu.VMEM((8, 128), I32),
            pltpu.SMEM((8, 128), I32),
            tile(8, 13),
            tile(8, 13),
            tile(4, 5),
            tile(4, 5),
            tile(),
            tile(COLS),
            pltpu.VMEM((16, 8, 256), F32),
            pltpu.VMEM((16, 1, 512), F32),
            pltpu.VMEM((8, 2, 16, 128), F32),
            pltpu.VMEM((COLS, 16, 128), F32),
            tile(COLS),
            tile(COLS),
            pltpu.VMEM((64, 416), BF16),
            pltpu.VMEM((64, 128), BF16),
            pltpu.VMEM((64, 128), BF16),
            pltpu.VMEM((2, 64, 128), BF16),
            pltpu.VMEM((128, D), BF16),
            pltpu.VMEM((64, D), BF16),
        ]
        + [dma] * 3
        + [dma((2,))]
        + [dma] * 10
        + [dma((9,)), dma, dma((4,))],
        compiler_params=pltpu.CompilerParams(
            collective_id=0, has_side_effects=True, vmem_limit_bytes=60 * 1024 * 1024
        ),
        name="mixer",
    )(
        ms, mt, cache_lengths, pt, dt_bias, a_log, d_skip,
        ms, mt, arrival.reshape(1, 416), norm_gain.reshape(1, 64), weight_dt.T, conv_weight_x, conv_weight_bc,
        conv_x.transpose(1, 0, 2), conv_bc.transpose(1, 0, 2),
        tokens.T, weight_z, weight_x, weight_bc, weight_qkv, weight_ssm_out, weight_attn_out,
        kv_pool.reshape(26, PAGE, 512), ssm_state.reshape(SLOTS, 128, NS),
    )
    kv_next, state_next, mixed, cx, cbc = pl.pallas_call(
        emit_kernel,
        out_shape=results,
        in_specs=[smem] * 2 + [anywhere] * 5,
        out_specs=(anywhere,) * 5,
        scratch_shapes=[pltpu.VMEM(m.shape, m.dtype) for m in made] + [dma((10,))],
        name="emit",
    )(ms, pt, *made)
    return (
        mixed,
        state_next.reshape(SLOTS, 2, HP, NS),
        cx.transpose(1, 0, 2),
        cbc.transpose(1, 0, 2),
        kv_next.reshape(26, 1, PAGE, 512),
    )


def solution(mesh):
    in_specs = (
        P(None, "rows"), P(), P(), P(), P(), P("rows", "cols", None, None), P("rows", "cols", None, None),
        P("rows", "cols", None, None), P("rows", None, "cols"), P("rows", None, None), P("rows"),
        P("rows", "cols"), P("rows", "cols"), P("rows", "cols"), P("rows", None), P("rows", None),
        P(None, "cols"), P(), P("cols"), P("cols"), P("cols"), P("cols", None), P("cols", None),
    )
    out_specs = (
        P("rows", "cols"),
        P("rows", "cols", None, None),
        P("rows", None, "cols"),
        P("rows", None, None),
        P("rows", "cols", None, None),
    )
    return jax.shard_map(local, mesh=mesh, in_specs=in_specs, out_specs=out_specs, check_vma=False)
```

```python
import jax
import jax.numpy as jnp
from jax import lax
from jax.experimental import pallas as pl
from jax.experimental.pallas import tpu as pltpu
from jax.sharding import PartitionSpec as P

D = 2048
HP = 64
NS = 256
HD = 128
PAGE = 32
SLOTS = 13
ROWS = 32
COLS = 16
MOVES = 4
EPSILON = 1e-05
FLOOR = -1e30
F32 = jnp.float32
BF16 = jnp.bfloat16
I32 = jnp.int32
MESH = pl.DeviceIdType.MESH


def nt(a, b):
    return lax.dot_general(a, b, (((1,), (1,)), ((), ())), preferred_element_type=F32)


def nn(a, b):
    return jnp.dot(a, b, preferred_element_type=F32)


def silu(v):
    return v / (1.0 + jnp.exp(-v))


def mixer_kernel(
    ms, mt, lengths, pt, dtb, alog, dskip,
    ms_v, mt_v, arrival, gain, wdt, cwx, cwbc, conv_x, conv_bc,
    tokens, wz, wx, wbc, wqkv, wssm, wattn, pool, state,
    kv_out, state_out, mixed_out, cx_out, cbc_out,
    send1, recv1, send2, recv2, pcomb, scomb, kvn, stn, leave, going, passing, came, table_v, table,
    send_r, recv_r, send_b, recv_b, send_s, recv_s, qbuf, fresh,
    send_a, recv_a, send_o, recv_o, tokens_v, wz_v, wx_v, shared_v, wssm_v, wattn_v,
    s1_sem, r1_sem, s2_sem, r2_sem, sr_sem, rr_sem, sb_sem, rb_sem, ss_sem, rs_sem,
    sa_sem, ra_sem, so_sem, ro_sem, in_sem, table_sem, out_sem,
):
    row = lax.axis_index("rows")
    col = lax.axis_index("cols")
    core = row & 1
    chip = row >> 1
    plane = row >> 3
    member = row & 7

    barrier = pltpu.get_barrier_semaphore()

    def greet_rows(d, carry):
        pl.semaphore_signal(barrier, inc=1, device_id=((row + d) & (ROWS - 1), col), device_id_type=MESH)
        return carry

    def greet_cols(d, carry):
        pl.semaphore_signal(barrier, inc=1, device_id=(row, (col + d) & (COLS - 1)), device_id_type=MESH)
        return carry

    loads = [
        pltpu.make_async_copy(src, dst, in_sem.at[i])
        for i, (src, dst) in enumerate((
            (tokens, tokens_v), (wz, wz_v), (wx, wx_v),
            (pool, pcomb.at[pl.ds(0, 26)]), (state, scomb.at[pl.ds(0, SLOTS)]),
            (wssm, wssm_v), (wattn, wattn_v),
        ))
    ]
    bc_at = pl.multiple_of(jnp.minimum(col, 3) * 128, 128)
    qkv_at = pl.multiple_of(jnp.maximum(col - 4, 0) * 128, 128)
    load_bc = pltpu.make_async_copy(wbc.at[:, pl.ds(bc_at, 128)], shared_v.at[0], in_sem.at[7])
    load_qkv = pltpu.make_async_copy(wqkv.at[:, pl.ds(qkv_at, 128)], shared_v.at[1], in_sem.at[8])
    for load in loads[3:5] + loads[:3] + [load_bc, load_qkv] + loads[5:]:
        load.start()
    lax.fori_loop(1, ROWS, greet_rows, 0)
    lax.fori_loop(1, COLS, greet_cols, 0)

    slots = [ms[m, row] for m in range(MOVES)]
    targets = [mt[m, row] for m in range(MOVES)]

    def cut_pages(m, carry):
        slot = ms[m, row]
        for page in range(2):
            g = pt[page, slot]
            for i in range(8):
                r, l = 16 * (i // 4), 128 * (i % 4)
                send1[2 * (8 * page + i), m] = pcomb[g, r : r + 16, l : l + 128]
        return carry

    loads[3].wait()
    lax.fori_loop(0, MOVES, cut_pages, 0)

    pl.semaphore_wait(barrier, ROWS + COLS - 2)

    def far_first(j, half):
        return half + jnp.where((j & 1) == 1, (j + 1) >> 1, -(j >> 1))

    def hop1(kind):
        def send(d, carry):
            to = 2 * ((chip + far_first(d, 8)) & 15) + kind

            @pl.when(to != row)
            def _():
                pltpu.make_async_remote_copy(
                    send1.at[to], recv1.at[(to - row) & (ROWS - 1)], s1_sem, r1_sem,
                    device_id=(to, col), device_id_type=MESH,
                ).start()

            return carry

        lax.fori_loop(0, 16, send, 0)

    hop1(0)

    def cut_states(m, carry):
        slot = ms[m, row]
        for p in range(16):
            r, l = 16 * (p // 2), 128 * (p % 2)
            send1[2 * p + 1, m] = scomb[slot, r : r + 16, l : l + 128]
        return carry

    loads[4].wait()
    lax.fori_loop(0, MOVES, cut_states, 0)

    lane = lax.broadcasted_iota(I32, (128, 128), 1)
    sub = lax.broadcasted_iota(I32, (128, 128), 0)
    eye = lane == sub
    line_ms = jnp.concatenate([ms_v[m : m + 1, :] for m in range(MOVES)], axis=1)
    line_mt = jnp.concatenate([mt_v[m : m + 1, :] for m in range(MOVES)], axis=1)
    wide = lambda v: jnp.broadcast_to(v, (128, 128))
    across = lambda v: jnp.sum(v, axis=1, keepdims=True)
    down = lambda v: jnp.sum(v, axis=0, keepdims=True)
    mt_col = across(jnp.where(eye, wide(line_mt), 0))
    ms_col = across(jnp.where(eye, wide(line_ms), 0))
    earlier = (sub & (ROWS - 1)) < (lane & (ROWS - 1))
    rank = down(jnp.where((wide(mt_col) == wide(line_mt)) & earlier, 1, 0))
    place = rank * ROWS + line_mt
    slot_there = down(jnp.where(sub == wide(place), wide(ms_col), 0))
    place_col = across(jnp.where(eye, wide(place), 0))
    kept_at = ((row - sub) & (ROWS - 1)) * 8 + (sub >> 5)
    table_v[...] = jnp.zeros_like(table_v)
    table_v[0:1, :] = down(jnp.where(wide(place_col) == lane, kept_at, 0))
    lane1 = lax.broadcasted_iota(I32, (1, 128), 1)
    owners = jnp.zeros((1, 128), I32)
    for s in range(SLOTS):
        for half in range(2):
            owners = jnp.where(lane1 == pt[half, s], 2 * s + half, owners)
    table_v[1:2, :] = owners
    load_table = pltpu.make_async_copy(table_v, table, table_sem)
    load_table.start()
    source_row = lane1 & (ROWS - 1)
    goes = 16 * line_mt + slot_there
    left = 16 * source_row + line_ms
    request = SLOTS * source_row + line_ms
    q = lax.broadcasted_iota(I32, (512, 128), 0)
    arrived = across(jnp.where(q == goes, request, 0))
    vacated = across(jnp.where(q == left, 1, 0))
    q1 = lax.broadcasted_iota(I32, (512, 1), 0)
    layout = jnp.where(vacated > 0, arrived, (q1 >> 4) * SLOTS + (q1 & 15))
    layout = jnp.where((q1 & 15) < SLOTS, layout, -1)

    onehot = jnp.where(layout == arrival[...], 1.0, 0.0).astype(BF16)
    loads[0].wait()
    picked = nt(onehot, tokens_v[...])
    scaled = (picked * gain[...].astype(F32)).astype(BF16)
    squares = jnp.square(picked)
    squares_hi = squares.astype(BF16)
    squares_lo = (squares - squares_hi.astype(F32)).astype(BF16)
    line64 = lax.broadcasted_iota(I32, (16, 64), 0)
    last = jnp.where(line64 == 15, 1.0, 0.0).astype(BF16)
    steps = wdt[...].astype(F32)
    steps = jnp.where(line64 == 13, steps[0:1], jnp.where(line64 == 14, steps[1:2], 0.0)).astype(BF16)
    extra = nt(steps, scaled) + nt(last, squares_hi) + nt(last, squares_lo)
    for load in (loads[1], loads[2], load_bc, load_qkv):
        load.wait()
    part_z = nn(scaled, wz_v[...]).reshape(4, 8, 16, 128)
    part_x = nn(scaled, wx_v[...]).reshape(4, 8, 16, 128).astype(BF16)
    part_s = nn(scaled, shared_v[jnp.where(col < 4, 0, 1)]).reshape(4, 8, 16, 128).astype(BF16)
    windows = [conv_x[k].astype(F32) for k in range(3)]
    windows += [conv_bc[k, :, 128 * c : 128 * (c + 1)].astype(F32) for k in range(3) for c in range(4)]
    lane16 = lax.broadcasted_iota(I32, (16, 128), 1)
    quarter = lane16 >> 5
    pad = jnp.zeros((3, 128), F32)
    bc_lanes = pl.ds(pl.multiple_of((col >> 2) * 128, 128), 128)
    taps = jnp.zeros((16, 128), F32)
    for k in range(3):
        tap = jnp.concatenate([conv_bc[k, :, bc_lanes].astype(F32), pad], axis=0)
        taps = jnp.where(quarter == k, pltpu.roll(tap, (32 * (k - (col & 3))) & 127, 1), taps)
        leave[:, k, :] = jnp.concatenate([windows[k], pad], axis=0)
    leave[:, 3, :] = taps

    def conv_rows(m, carry):
        for u in range(4):
            at = slots[0]
            for k in range(1, MOVES):
                at = jnp.where(targets[k] == 8 * u + m, slots[k], at)
            going[m, 4 * u : 4 * u + 4, :] = leave[at][0:4]
        return carry

    lax.fori_loop(0, 8, conv_rows, 0)
    send_r[:, 12] = going[...].astype(BF16)
    for u in range(4):
        send_r[:, 3 * u] = (part_z[u] + extra[:, 128 * u : 128 * (u + 1)][None]).astype(BF16)
        send_r[:, 3 * u + 1] = part_x[u]
        send_r[:, 3 * u + 2] = part_s[u]

    def reduce_in(d, carry):
        to = (member + d) & 7
        pltpu.make_async_remote_copy(
            send_r.at[to], recv_r.at[d], sr_sem, rr_sem, device_id=(plane * 8 + to, col), device_id_type=MESH
        ).start()
        return carry

    lax.fori_loop(1, 8, reduce_in, 0)

    @pl.when(core == 1)
    def _():
        hop1(1)

    recv_r[0] = send_r[member]

    load_table.wait()

    away_r = recv_r.at[pl.ds(1, 7)]
    pltpu.make_async_copy(away_r, away_r, rr_sem).wait()
    for u in range(4):
        for j in range(3):
            total = recv_r[0, 3 * u + j].astype(F32)
            for d in range(1, 8):
                total = total + recv_r[d, 3 * u + j].astype(F32)
            send_b[u, j] = total.astype(BF16)
    for d in range(8):
        rows_d = recv_r[d, 12].astype(F32)
        for u in range(4):
            passing[u, 4 * d : 4 * d + 4, :] = rows_d[4 * u : 4 * u + 4]
    for u in range(4):
        send_b[u, 3] = passing[u, 0:16].astype(BF16)
        send_b[u, 4] = passing[u, 16:32].astype(BF16)

    def reduce_across(d, carry):
        to = (plane + d) & 3
        pltpu.make_async_remote_copy(
            send_b.at[to], recv_b.at[d], sb_sem, rb_sem, device_id=(to * 8 + member, col), device_id_type=MESH
        ).start()
        return carry

    lax.fori_loop(1, 4, reduce_across, 0)

    away1 = recv1.at[pl.ds(1, ROWS - 1)]

    def pick(t, carry):
        for k in range(MOVES):
            code = table[0, ROWS * k + t]
            send2[t, k] = recv1[(code >> 3) & (ROWS - 1), code & 3]
        return carry

    def hop2(j, carry):
        d = far_first(j, 16)
        to = (row + d) & (ROWS - 1)
        pick(to, carry)
        pltpu.make_async_remote_copy(
            send2.at[to], recv2.at[d], s2_sem, r2_sem.at[core], device_id=(to, col), device_id_type=MESH
        ).start()
        return carry

    def second_hop(kind):
        @pl.when(core == kind)
        def _():
            recv1[0] = send1[row]
            pltpu.make_async_copy(away1, away1, r1_sem).wait()
            lax.fori_loop(0, ROWS - 1, hop2, 0)
            pick(row, 0)
            recv2[0] = send2[row]

    second_hop(0)

    @pl.when(core == 0)
    def _():
        hop1(1)

    recv_b[0] = send_b[plane]
    away_b = recv_b.at[pl.ds(1, 3)]
    pltpu.make_async_copy(away_b, away_b, rb_sem).wait()

    zero = jnp.zeros((16, 128), F32)
    sum_z, sum_x, sum_s = (
        recv_b[0, j].astype(F32) + recv_b[1, j].astype(F32) + recv_b[2, j].astype(F32) + recv_b[3, j].astype(F32)
        for j in range(3)
    )
    lane = lax.broadcasted_iota(I32, (16, 128), 1)
    sub = lax.broadcasted_iota(I32, (16, 128), 0)
    low = lane < HP
    mine = lane == sub + 16 * member

    def as_column(k):
        return jnp.sum(jnp.where(mine, jnp.broadcast_to(sum_z[k : k + 1], (16, 128)), 0.0), axis=1, keepdims=True)

    root = jnp.sqrt(as_column(15) / D + EPSILON)
    real = sub < SLOTS
    gate_in = jnp.where(real, sum_z / root, 0.0).astype(BF16).astype(F32)
    value_in = jnp.where(real, sum_x / root, 0.0).astype(BF16)
    step_in = jnp.where(low, as_column(13) / root, as_column(14) / root).astype(BF16).astype(F32)

    for e in range(4):
        for half in range(2):
            rows_e = recv_b[e, 3 + half].astype(F32)
            for d in range(4):
                came[8 * e + 4 * half + d, 0:4, :] = rows_e[4 * d : 4 * d + 4]
    codes = [table[0, ROWS * k + row] for k in range(MOVES)]
    tiles = []
    for code in codes:
        at = (row - (code >> 3)) & (ROWS - 1)
        tiles.append(came[8 * ((plane - (at >> 3)) & 3) + ((member - (at & 7)) & 7)])
    quarter = lane >> 5
    bc_rows = zero
    for k in range(3):
        for m in range(MOVES):
            moved = jnp.broadcast_to(tiles[m][3:4], (16, 128))
            moved = moved if m == k else pltpu.roll(moved, (32 * (m - k)) % 128, 1)
            bc_rows = jnp.where((sub == SLOTS + k) & (quarter == m), moved, bc_rows)
    send_s[...] = jnp.where(real, sum_s / root, bc_rows).astype(BF16)

    def share(j, carry):
        d = far_first(j, 8)
        to = (col + d) & (COLS - 1)
        pltpu.make_async_remote_copy(
            send_s, recv_s.at[d], ss_sem, rs_sem, device_id=(row, to), device_id_type=MESH
        ).start()
        return carry

    lax.fori_loop(0, COLS - 1, share, 0)
    recv_s[0] = send_s[...]

    second_hop(1)

    def wait_pieces(kind):
        @pl.when(core == kind)
        def _():
            some = recv2.at[pl.ds(0, 15)]
            pltpu.make_async_copy(some, some, r2_sem.at[kind]).wait()

        @pl.when(core != kind)
        def _():
            some = recv2.at[pl.ds(0, 16)]
            pltpu.make_async_copy(some, some, r2_sem.at[kind]).wait()

    def with_arrived(i, rows_of):
        rows_i = jnp.concatenate([windows[i], jnp.zeros((3, 128), F32)], axis=0)
        for k in range(MOVES):
            rows_i = jnp.where(sub == slots[k], jnp.broadcast_to(rows_of(k), (16, 128)), rows_i)
        return rows_i

    window = [with_arrived(i, lambda k, i=i: tiles[k][i : i + 1]) for i in range(3)]

    taps_x = cwx[...].astype(F32)
    taps_bc = cwbc[...].astype(F32)
    conv = value_in.astype(F32) * taps_x[3:4]
    for k in range(3):
        conv = conv + window[k] * taps_x[k : k + 1]
    value_act = silu(conv)
    cx_out[0] = window[1][:SLOTS].astype(BF16)
    cx_out[1] = window[2][:SLOTS].astype(BF16)
    cx_out[2] = value_in[:SLOTS]
    head_lanes = lambda ref: jnp.where(low, ref[0], ref[1])
    raw_step = step_in + head_lanes(dtb)
    step = jnp.maximum(raw_step, 0.0) + jnp.log1p(jnp.exp(-jnp.abs(raw_step)))
    decay = jnp.exp(-jnp.exp(head_lanes(alog)) * step)
    grown = step * value_act

    away_s = recv_s.at[pl.ds(1, COLS - 1)]
    pltpu.make_async_copy(away_s, away_s, rs_sem).wait()

    def chunk(c):
        return recv_s[(col - c) & (COLS - 1)]

    for c in range(4):
        joined = []
        for m in range(MOVES):
            rows_m = zero
            for j in range(4):
                other = chunk(4 * c + j).astype(F32)
                other = other if j == m else pltpu.roll(other, (32 * (j - m)) % 128, 1)
                rows_m = jnp.where(quarter == j, other, rows_m)
            joined.append(rows_m)
        window += [
            with_arrived(3 + 4 * k + c, lambda m, k=k: joined[m][SLOTS + k : SLOTS + k + 1]) for k in range(3)
        ]
    act = []
    for c in range(4):
        new = chunk(c)
        lanes = slice(128 * c, 128 * (c + 1))
        conv = new.astype(F32) * taps_bc[3:4, lanes]
        for k in range(3):
            conv = conv + window[3 + 3 * c + k] * taps_bc[k : k + 1, lanes]
        act.append(silu(conv).astype(BF16))
        cbc_out[0, :, lanes] = window[3 + 3 * c + 1][:SLOTS].astype(BF16)
        cbc_out[1, :, lanes] = window[3 + 3 * c + 2][:SLOTS].astype(BF16)
        cbc_out[2, :, lanes] = new[:SLOTS]
    b_in = jnp.concatenate(act[:2], axis=1)
    c_out = jnp.concatenate(act[2:], axis=1)

    qbuf[...] = jnp.zeros_like(qbuf)
    for h in range(8):
        lanes = slice(128 * (h // 4), 128 * (h // 4 + 1))
        qbuf[:, h, lanes] = chunk(4 + h).astype(F32)
    for j in range(4):
        fresh[:, 0, 128 * j : 128 * (j + 1)] = chunk(12 + j).astype(F32)

    def length_of(s):
        request = row * SLOTS + s
        for k in range(MOVES):
            at = (row - (codes[k] >> 3)) & (ROWS - 1)
            request = jnp.where(slots[k] == s, at * SLOTS + ms[codes[k] & 3, at], request)
        return lengths[request]

    line = lax.broadcasted_iota(I32, (PAGE, 512), 0)

    def page(at, s, half):
        length = length_of(s)
        logical = length >> 5
        here = ((logical & (COLS - 1)) == col) & ((logical >> 4) == half)
        offset = jnp.where(here, length & (PAGE - 1), -1)
        return jnp.where(line == offset, fresh[s].astype(F32), pcomb[at].astype(F32)).astype(BF16)

    def own_page(g, carry):
        entry = table[1, g]
        kvn[g] = page(g, entry >> 1, entry & 1)
        return carry

    lax.fori_loop(0, 26, own_page, 0)
    kv_copy = pltpu.make_async_copy(kvn.at[pl.ds(0, 26)], kv_out.at[pl.ds(0, 26)], out_sem.at[0])
    kv_copy.start()

    token = lax.broadcasted_iota(I32, (8, 64), 1)
    position = (token >> 5) * (COLS * PAGE) + col * PAGE + (token & (PAGE - 1))
    head = lax.broadcasted_iota(I32, (8, 128), 0)
    lane8 = lax.broadcasted_iota(I32, (8, 128), 1)

    def attention(s, first, second):
        both = jnp.concatenate([first, second], axis=0)
        scores = nt(qbuf[s].astype(BF16), both[:, :256]) * (HD**-0.5)
        live = position <= length_of(s)
        peak = jnp.max(jnp.where(live, scores, FLOOR), axis=1, keepdims=True)
        weights = jnp.where(live, jnp.exp(scores - peak), 0.0)
        summed = nn(weights.astype(BF16), both[:, 256:])
        summed = jnp.where(head < 4, summed[:, :128], summed[:, 128:])
        stats = jnp.where(lane8 == HP, peak, jnp.sum(weights, axis=1, keepdims=True))
        return jnp.where(lane8 < HP, summed, stats), jnp.where(lane8 < HP, pltpu.roll(summed, HP, 1), stats)

    for s in range(SLOTS):
        send_a[:, 0, s, :], send_a[:, 1, s, :] = attention(s, kvn[pt[0, s]], kvn[pt[1, s]])
    for s in range(SLOTS, 16):
        send_a[:, 0, s, :] = jnp.zeros((8, 128), F32)
        send_a[:, 1, s, :] = jnp.zeros((8, 128), F32)

    wait_pieces(0)

    def paste_pages(k, carry):
        for p in range(16):
            i = p % 8
            r, l = 16 * (i // 4), 128 * (i % 4)
            pcomb[26 + 2 * k + p // 8, r : r + 16, l : l + 128] = recv2[(row - 2 * p) & (ROWS - 1), k]
        for half in range(2):
            kvn[26 + 2 * k + half] = page(26 + 2 * k + half, ms[k, row], half)
        return carry

    lax.fori_loop(0, MOVES, paste_pages, 0)
    kv_copy2 = pltpu.make_async_copy(kvn.at[pl.ds(26, 8)], kv_out.at[pl.ds(26, 8)], out_sem.at[1])
    kv_copy2.start()
    found = [attention(slots[k], kvn[26 + 2 * k], kvn[27 + 2 * k]) for k in range(MOVES)]
    for h in range(8):
        for half in range(2):
            tile = send_a[h, half]
            for k in range(MOVES):
                tile = jnp.where(sub == slots[k], jnp.broadcast_to(found[k][half][h : h + 1], (16, 128)), tile)
            send_a[h, half] = tile

    def attend(j, carry):
        d = far_first(j, 8)
        to = (col + d) & (COLS - 1)
        pltpu.make_async_remote_copy(
            send_a.at[to >> 1, to & 1], recv_a.at[d], sa_sem, ra_sem, device_id=(row, to), device_id_type=MESH
        ).start()
        return carry

    lax.fori_loop(0, COLS - 1, attend, 0)
    recv_a[0] = send_a[col >> 1, col & 1]

    read = zero
    for s in range(SLOTS):
        read = jnp.where(sub == s, nt(c_out, scomb[s]), read)
    columns = jnp.concatenate([grown, decay, jnp.zeros((96, 128), F32)], axis=0).T
    for s in range(SLOTS):
        old = scomb[s].astype(F32)
        new = columns[:, 16 + s : 17 + s] * old + columns[:, s : s + 1] * b_in[s : s + 1].astype(F32)
        stn[s] = new.astype(BF16)
    own_states = pl.ds(0, SLOTS)
    state_copy_out = pltpu.make_async_copy(stn.at[own_states], state_out.at[own_states], out_sem.at[2])
    state_copy_out.start()
    b_dot_c = jnp.sum(b_in.astype(F32) * c_out.astype(F32), axis=1, keepdims=True)
    loads[5].wait()
    loads[6].wait()

    wait_pieces(1)

    def paste_states(k, carry):
        for p in range(16):
            r, l = 16 * (p // 2), 128 * (p % 2)
            scomb[SLOTS + k, r : r + 16, l : l + 128] = recv2[(row - 2 * p - 1) & (ROWS - 1), k]
        return carry

    lax.fori_loop(0, MOVES, paste_states, 0)
    for k in range(MOVES):
        read = jnp.where(sub == slots[k], nt(c_out, scomb[SLOTS + k]), read)
    readout = decay * read + grown * b_dot_c + head_lanes(dskip) * value_act
    gated = (readout * silu(gate_in)).astype(BF16)
    out_terms = nn(gated, wssm_v[...])

    away_a = recv_a.at[pl.ds(1, COLS - 1)]
    pltpu.make_async_copy(away_a, away_a, ra_sem).wait()
    top = recv_a[0]
    for d in range(1, COLS):
        top = jnp.maximum(top, recv_a[d])
    top = top[:, HP : HP + 1]
    gathered = zero
    for d in range(COLS):
        part = recv_a[d]
        gathered = gathered + part * jnp.exp(part[:, HP : HP + 1] - top)
    attended = jnp.where(real, gathered / gathered[:, HP + 1 : HP + 2], 0.0).astype(BF16)
    out_terms = out_terms + nn(attended[:, :HP], wattn_v[...])
    for c in range(COLS):
        send_o[c] = out_terms[:, 128 * c : 128 * (c + 1)].astype(BF16)

    def project(j, carry):
        d = far_first(j, 8)
        to = (col + d) & (COLS - 1)
        pltpu.make_async_remote_copy(
            send_o.at[to], recv_o.at[d], so_sem, ro_sem, device_id=(row, to), device_id_type=MESH
        ).start()
        return carry

    lax.fori_loop(0, COLS - 1, project, 0)
    recv_o[0] = send_o[col]

    lanes = lax.broadcasted_iota(I32, (128, 128), 1)
    rows_b = lax.broadcasted_iota(I32, (16, 256), 0)
    for k in range(MOVES):
        up = jnp.sum(jnp.where(lanes == slots[k], columns, 0.0), axis=1, keepdims=True)
        down_by = jnp.sum(jnp.where(lanes == slots[k] + 16, columns, 0.0), axis=1, keepdims=True)
        b_row = jnp.sum(jnp.where(rows_b == slots[k], b_in.astype(F32), 0.0), axis=0, keepdims=True)
        stn[SLOTS + k] = (down_by * scomb[SLOTS + k].astype(F32) + up * b_row).astype(BF16)
    new_states = pl.ds(SLOTS, MOVES)
    state_copy2 = pltpu.make_async_copy(stn.at[new_states], state_out.at[new_states], out_sem.at[3])
    state_copy2.start()

    away_o = recv_o.at[pl.ds(1, COLS - 1)]
    pltpu.make_async_copy(away_o, away_o, ro_sem).wait()
    mixed = zero
    for d in range(COLS):
        mixed = mixed + recv_o[d].astype(F32)
    mixed_out[...] = mixed[:SLOTS].astype(BF16)

    sent1 = send1.at[pl.ds(0, ROWS - 1)]
    pltpu.make_async_copy(sent1, sent1, s1_sem).wait()
    sent2 = send2.at[pl.ds(0, ROWS - 1)]
    pltpu.make_async_copy(sent2, sent2, s2_sem).wait()
    sent_r = send_r.at[pl.ds(0, 7)]
    pltpu.make_async_copy(sent_r, sent_r, sr_sem).wait()
    sent_b = send_b.at[pl.ds(0, 3)]
    pltpu.make_async_copy(sent_b, sent_b, sb_sem).wait()
    for sem, ref in ((ss_sem, recv_s), (sa_sem, recv_a), (so_sem, send_o)):
        sent = ref.at[pl.ds(0, COLS - 1)]
        pltpu.make_async_copy(sent, sent, sem).wait()
    for copy in (kv_copy, kv_copy2, state_copy_out, state_copy2):
        copy.wait()


def emit_kernel(ms, pt, *refs):
    made, out, held, sem = refs[:5], refs[5:10], refs[10:15], refs[15]
    row = lax.axis_index("rows")
    ready = list(held)
    ready[0] = held[0].at[pl.ds(0, 26)]
    ready[1] = held[1].at[pl.ds(0, SLOTS)]
    reads = [pltpu.make_async_copy(made[i], held[i], sem.at[i]) for i in range(5)]
    writes = [pltpu.make_async_copy(ready[i], out[i], sem.at[5 + i]) for i in range(5)]
    for read in reads:
        read.start()
    for i in (2, 3, 4, 0, 1):
        reads[i].wait()
        for k in range(MOVES):
            slot = ms[k, row]
            if i == 0:
                held[0][pt[0, slot]] = held[0][26 + 2 * k]
                held[0][pt[1, slot]] = held[0][27 + 2 * k]
            if i == 1:
                held[1][slot] = held[1][SLOTS + k]
        writes[i].start()
    for write in writes:
        write.wait()


def local(
    tokens, arrival, cache_lengths, move_slot, move_target, page_table, kv_pool, ssm_state, conv_x, conv_bc,
    norm_gain, weight_z, weight_x, weight_dt, weight_bc, weight_qkv, conv_weight_x, conv_weight_bc,
    dt_bias, a_log, d_skip, weight_ssm_out, weight_attn_out,
):
    vmem = pl.BlockSpec(memory_space=pltpu.VMEM)
    smem = pl.BlockSpec(memory_space=pltpu.SMEM)
    anywhere = pl.BlockSpec(memory_space=pl.ANY)
    ms, mt = move_slot.T, move_target.T
    pt = page_table.reshape(SLOTS, 2).T
    dma = pltpu.SemaphoreType.DMA
    results = (
        jax.ShapeDtypeStruct((26, PAGE, 512), BF16),
        jax.ShapeDtypeStruct((SLOTS, 128, NS), BF16),
        jax.ShapeDtypeStruct((SLOTS, 128), BF16),
        jax.ShapeDtypeStruct((3, SLOTS, 128), BF16),
        jax.ShapeDtypeStruct((3, SLOTS, 512), BF16),
    )
    tile = lambda *lead: pltpu.VMEM((*lead, 16, 128), BF16)
    made = pl.pallas_call(
        mixer_kernel,
        out_shape=(
            jax.ShapeDtypeStruct((34, PAGE, 512), BF16),
            jax.ShapeDtypeStruct((SLOTS + MOVES, 128, NS), BF16),
            *results[2:],
        ),
        in_specs=[smem] * 7 + [vmem] * 9 + [anywhere] * 9,
        out_specs=(anywhere, anywhere, vmem, vmem, vmem),
        scratch_shapes=[
            tile(ROWS, MOVES),
            tile(ROWS, MOVES),
            tile(ROWS, MOVES),
            tile(ROWS, MOVES),
            pltpu.VMEM((34, PAGE, 512), BF16),
            pltpu.VMEM((SLOTS + MOVES, 128, NS), BF16),
            pltpu.VMEM((34, PAGE, 512), BF16),
            pltpu.VMEM((SLOTS + MOVES, 128, NS), BF16),
            pltpu.VMEM((16, 8, 128), F32),
            pltpu.VMEM((8, 16, 128), F32),
            pltpu.VMEM((4, 32, 128), F32),
            pltpu.VMEM((ROWS, 8, 128), F32),
            pltpu.VMEM((8, 128), I32),
            pltpu.SMEM((8, 128), I32),
            tile(8, 13),
            tile(8, 13),
            tile(4, 5),
            tile(4, 5),
            tile(),
            tile(COLS),
            pltpu.VMEM((16, 8, 256), F32),
            pltpu.VMEM((16, 1, 512), F32),
            pltpu.VMEM((8, 2, 16, 128), F32),
            pltpu.VMEM((COLS, 16, 128), F32),
            tile(COLS),
            tile(COLS),
            pltpu.VMEM((64, 416), BF16),
            pltpu.VMEM((64, 128), BF16),
            pltpu.VMEM((64, 128), BF16),
            pltpu.VMEM((2, 64, 128), BF16),
            pltpu.VMEM((128, D), BF16),
            pltpu.VMEM((64, D), BF16),
        ]
        + [dma] * 3
        + [dma((2,))]
        + [dma] * 10
        + [dma((9,)), dma, dma((4,))],
        compiler_params=pltpu.CompilerParams(
            collective_id=0, has_side_effects=True, vmem_limit_bytes=60 * 1024 * 1024
        ),
        name="mixer",
    )(
        ms, mt, cache_lengths, pt, dt_bias, a_log, d_skip,
        ms, mt, arrival.reshape(1, 416), norm_gain.reshape(1, 64), weight_dt.T, conv_weight_x, conv_weight_bc,
        conv_x.transpose(1, 0, 2), conv_bc.transpose(1, 0, 2),
        tokens.T, weight_z, weight_x, weight_bc, weight_qkv, weight_ssm_out, weight_attn_out,
        kv_pool.reshape(26, PAGE, 512), ssm_state.reshape(SLOTS, 128, NS),
    )
    kv_next, state_next, mixed, cx, cbc = pl.pallas_call(
        emit_kernel,
        out_shape=results,
        in_specs=[smem] * 2 + [anywhere] * 5,
        out_specs=(anywhere,) * 5,
        scratch_shapes=[pltpu.VMEM(m.shape, m.dtype) for m in made] + [dma((10,))],
        name="emit",
    )(ms, pt, *made)
    return (
        mixed,
        state_next.reshape(SLOTS, 2, HP, NS),
        cx.transpose(1, 0, 2),
        cbc.transpose(1, 0, 2),
        kv_next.reshape(26, 1, PAGE, 512),
    )


def solution(mesh):
    in_specs = (
        P(None, "rows"), P(), P(), P(), P(), P("rows", "cols", None, None), P("rows", "cols", None, None),
        P("rows", "cols", None, None), P("rows", None, "cols"), P("rows", None, None), P("rows"),
        P("rows", "cols"), P("rows", "cols"), P("rows", "cols"), P("rows", None), P("rows", None),
        P(None, "cols"), P(), P("cols"), P("cols"), P("cols"), P("cols", None), P("cols", None),
    )
    out_specs = (
        P("rows", "cols"),
        P("rows", "cols", None, None),
        P("rows", None, "cols"),
        P("rows", None, None),
        P("rows", "cols", None, None),
    )
    return jax.shard_map(local, mesh=mesh, in_specs=in_specs, out_specs=out_specs, check_vma=False)
```

```python
import jax
import jax.numpy as jnp
from jax import lax
from jax.experimental import pallas as pl
from jax.experimental.pallas import tpu as pltpu
from jax.sharding import PartitionSpec as P

D = 2048
HP = 64
NS = 256
HD = 128
PAGE = 32
SLOTS = 13
ROWS = 32
COLS = 16
MOVES = 4
EPSILON = 1e-05
FLOOR = -1e30
F32 = jnp.float32
BF16 = jnp.bfloat16
I32 = jnp.int32
MESH = pl.DeviceIdType.MESH


def nt(a, b):
    return lax.dot_general(a, b, (((1,), (1,)), ((), ())), preferred_element_type=F32)


def nn(a, b):
    return jnp.dot(a, b, preferred_element_type=F32)


def silu(v):
    return v / (1.0 + jnp.exp(-v))


def mixer_kernel(
    ms, mt, lengths, pt, dtb, alog, dskip,
    ms_v, mt_v, arrival, gain, wdt, cwx, cwbc, conv_x, conv_bc,
    tokens, wz, wx, wbc, wqkv, wssm, wattn, pool, state,
    kv_out, state_out, mixed_out, cx_out, cbc_out,
    send1, recv1, send2, recv2, pcomb, scomb, kvn, stn, leave, going, passing, came, table_v, table,
    send_r, recv_r, send_b, recv_b, send_s, recv_s, qbuf, fresh,
    send_a, leave_a, recv_a, send_o, recv_o, tokens_v, wz_v, wx_v, shared_v, wssm_v, wattn_v,
    s1_sem, r1_sem, s2_sem, r2_sem, sr_sem, rr_sem, sb_sem, rb_sem, ss_sem, rs_sem,
    sa_sem, ra_sem, so_sem, ro_sem, in_sem, table_sem, out_sem,
):
    row = lax.axis_index("rows")
    col = lax.axis_index("cols")
    core = row & 1
    chip = row >> 1
    plane = row >> 3
    member = row & 7

    barrier = pltpu.get_barrier_semaphore()

    def greet_rows(d, carry):
        pl.semaphore_signal(barrier, inc=1, device_id=((row + d) & (ROWS - 1), col), device_id_type=MESH)
        return carry

    def greet_cols(d, carry):
        pl.semaphore_signal(barrier, inc=1, device_id=(row, (col + d) & (COLS - 1)), device_id_type=MESH)
        return carry

    loads = [
        pltpu.make_async_copy(src, dst, in_sem.at[i])
        for i, (src, dst) in enumerate((
            (tokens, tokens_v), (wz, wz_v), (wx, wx_v),
            (pool, pcomb.at[pl.ds(0, 26)]), (state, scomb.at[pl.ds(0, SLOTS)]),
            (wssm, wssm_v), (wattn, wattn_v),
        ))
    ]
    bc_at = pl.multiple_of(jnp.minimum(col, 3) * 128, 128)
    qkv_at = pl.multiple_of(jnp.maximum(col - 4, 0) * 128, 128)
    load_bc = pltpu.make_async_copy(wbc.at[:, pl.ds(bc_at, 128)], shared_v.at[0], in_sem.at[7])
    load_qkv = pltpu.make_async_copy(wqkv.at[:, pl.ds(qkv_at, 128)], shared_v.at[1], in_sem.at[8])
    for load in loads[3:5] + loads[:3] + [load_bc, load_qkv] + loads[5:]:
        load.start()
    lax.fori_loop(1, ROWS, greet_rows, 0)
    lax.fori_loop(1, COLS, greet_cols, 0)

    slots = [ms[m, row] for m in range(MOVES)]
    targets = [mt[m, row] for m in range(MOVES)]

    def cut_pages(m, carry):
        slot = ms[m, row]
        for page in range(2):
            g = pt[page, slot]
            for i in range(8):
                r, l = 16 * (i // 4), 128 * (i % 4)
                send1[2 * (8 * page + i), m] = pcomb[g, r : r + 16, l : l + 128]
        return carry

    loads[3].wait()
    lax.fori_loop(0, MOVES, cut_pages, 0)

    pl.semaphore_wait(barrier, ROWS + COLS - 2)

    def far_first(j, half):
        return half + jnp.where((j & 1) == 1, (j + 1) >> 1, -(j >> 1))

    def hop1(kind):
        def send(d, carry):
            to = 2 * ((chip + far_first(d, 8)) & 15) + kind

            @pl.when(to != row)
            def _():
                pltpu.make_async_remote_copy(
                    send1.at[to], recv1.at[(to - row) & (ROWS - 1)], s1_sem, r1_sem,
                    device_id=(to, col), device_id_type=MESH,
                ).start()

            return carry

        lax.fori_loop(0, 16, send, 0)

    hop1(0)

    def cut_states(m, carry):
        slot = ms[m, row]
        for p in range(16):
            r, l = 16 * (p // 2), 128 * (p % 2)
            send1[2 * p + 1, m] = scomb[slot, r : r + 16, l : l + 128]
        return carry

    loads[4].wait()
    lax.fori_loop(0, MOVES, cut_states, 0)

    lane = lax.broadcasted_iota(I32, (128, 128), 1)
    sub = lax.broadcasted_iota(I32, (128, 128), 0)
    eye = lane == sub
    line_ms = jnp.concatenate([ms_v[m : m + 1, :] for m in range(MOVES)], axis=1)
    line_mt = jnp.concatenate([mt_v[m : m + 1, :] for m in range(MOVES)], axis=1)
    wide = lambda v: jnp.broadcast_to(v, (128, 128))
    across = lambda v: jnp.sum(v, axis=1, keepdims=True)
    down = lambda v: jnp.sum(v, axis=0, keepdims=True)
    mt_col = across(jnp.where(eye, wide(line_mt), 0))
    ms_col = across(jnp.where(eye, wide(line_ms), 0))
    earlier = (sub & (ROWS - 1)) < (lane & (ROWS - 1))
    rank = down(jnp.where((wide(mt_col) == wide(line_mt)) & earlier, 1, 0))
    place = rank * ROWS + line_mt
    slot_there = down(jnp.where(sub == wide(place), wide(ms_col), 0))
    place_col = across(jnp.where(eye, wide(place), 0))
    kept_at = ((row - sub) & (ROWS - 1)) * 8 + (sub >> 5)
    table_v[...] = jnp.zeros_like(table_v)
    table_v[0:1, :] = down(jnp.where(wide(place_col) == lane, kept_at, 0))
    lane1 = lax.broadcasted_iota(I32, (1, 128), 1)
    owners = jnp.zeros((1, 128), I32)
    for s in range(SLOTS):
        for half in range(2):
            owners = jnp.where(lane1 == pt[half, s], 2 * s + half, owners)
    table_v[1:2, :] = owners
    load_table = pltpu.make_async_copy(table_v, table, table_sem)
    load_table.start()
    source_row = lane1 & (ROWS - 1)
    goes = 16 * line_mt + slot_there
    left = 16 * source_row + line_ms
    request = SLOTS * source_row + line_ms
    q = lax.broadcasted_iota(I32, (512, 128), 0)
    arrived = across(jnp.where(q == goes, request, 0))
    vacated = across(jnp.where(q == left, 1, 0))
    q1 = lax.broadcasted_iota(I32, (512, 1), 0)
    layout = jnp.where(vacated > 0, arrived, (q1 >> 4) * SLOTS + (q1 & 15))
    layout = jnp.where((q1 & 15) < SLOTS, layout, -1)

    onehot = jnp.where(layout == arrival[...], 1.0, 0.0).astype(BF16)
    loads[0].wait()
    picked = nt(onehot, tokens_v[...])
    scaled = (picked * gain[...].astype(F32)).astype(BF16)
    squares = jnp.square(picked)
    squares_hi = squares.astype(BF16)
    squares_lo = (squares - squares_hi.astype(F32)).astype(BF16)
    line64 = lax.broadcasted_iota(I32, (16, 64), 0)
    last = jnp.where(line64 == 15, 1.0, 0.0).astype(BF16)
    steps = wdt[...].astype(F32)
    steps = jnp.where(line64 == 13, steps[0:1], jnp.where(line64 == 14, steps[1:2], 0.0)).astype(BF16)
    extra = nt(steps, scaled) + nt(last, squares_hi) + nt(last, squares_lo)
    for load in (loads[1], loads[2], load_bc, load_qkv):
        load.wait()
    part_z = nn(scaled, wz_v[...]).reshape(4, 8, 16, 128)
    part_x = nn(scaled, wx_v[...]).reshape(4, 8, 16, 128).astype(BF16)
    part_s = nn(scaled, shared_v[jnp.where(col < 4, 0, 1)]).reshape(4, 8, 16, 128).astype(BF16)
    windows = [conv_x[k].astype(F32) for k in range(3)]
    windows += [conv_bc[k, :, 128 * c : 128 * (c + 1)].astype(F32) for k in range(3) for c in range(4)]
    lane16 = lax.broadcasted_iota(I32, (16, 128), 1)
    quarter = lane16 >> 5
    pad = jnp.zeros((3, 128), F32)
    bc_lanes = pl.ds(pl.multiple_of((col >> 2) * 128, 128), 128)
    taps = jnp.zeros((16, 128), F32)
    for k in range(3):
        tap = jnp.concatenate([conv_bc[k, :, bc_lanes].astype(F32), pad], axis=0)
        taps = jnp.where(quarter == k, pltpu.roll(tap, (32 * (k - (col & 3))) & 127, 1), taps)
        leave[:, k, :] = jnp.concatenate([windows[k], pad], axis=0)
    leave[:, 3, :] = taps

    def conv_rows(m, carry):
        for u in range(4):
            at = slots[0]
            for k in range(1, MOVES):
                at = jnp.where(targets[k] == 8 * u + m, slots[k], at)
            going[m, 4 * u : 4 * u + 4, :] = leave[at][0:4]
        return carry

    lax.fori_loop(0, 8, conv_rows, 0)
    send_r[:, 12] = going[...].astype(BF16)
    for u in range(4):
        send_r[:, 3 * u] = (part_z[u] + extra[:, 128 * u : 128 * (u + 1)][None]).astype(BF16)
        send_r[:, 3 * u + 1] = part_x[u]
        send_r[:, 3 * u + 2] = part_s[u]

    def reduce_in(d, carry):
        to = (member + d) & 7
        pltpu.make_async_remote_copy(
            send_r.at[to], recv_r.at[d], sr_sem, rr_sem, device_id=(plane * 8 + to, col), device_id_type=MESH
        ).start()
        return carry

    lax.fori_loop(1, 8, reduce_in, 0)

    @pl.when(core == 1)
    def _():
        hop1(1)

    recv_r[0] = send_r[member]

    load_table.wait()

    away_r = recv_r.at[pl.ds(1, 7)]
    pltpu.make_async_copy(away_r, away_r, rr_sem).wait()
    for u in range(4):
        for j in range(3):
            total = recv_r[0, 3 * u + j].astype(F32)
            for d in range(1, 8):
                total = total + recv_r[d, 3 * u + j].astype(F32)
            send_b[u, j] = total.astype(BF16)
    for d in range(8):
        rows_d = recv_r[d, 12].astype(F32)
        for u in range(4):
            passing[u, 4 * d : 4 * d + 4, :] = rows_d[4 * u : 4 * u + 4]
    for u in range(4):
        send_b[u, 3] = passing[u, 0:16].astype(BF16)
        send_b[u, 4] = passing[u, 16:32].astype(BF16)

    def reduce_across(d, carry):
        to = (plane + d) & 3
        pltpu.make_async_remote_copy(
            send_b.at[to], recv_b.at[d], sb_sem, rb_sem, device_id=(to * 8 + member, col), device_id_type=MESH
        ).start()
        return carry

    lax.fori_loop(1, 4, reduce_across, 0)

    away1 = recv1.at[pl.ds(1, ROWS - 1)]

    def pick(t, carry):
        for k in range(MOVES):
            code = table[0, ROWS * k + t]
            send2[t, k] = recv1[(code >> 3) & (ROWS - 1), code & 3]
        return carry

    def hop2(j, carry):
        d = far_first(j, 16)
        to = (row + d) & (ROWS - 1)
        pick(to, carry)
        pltpu.make_async_remote_copy(
            send2.at[to], recv2.at[d], s2_sem, r2_sem.at[core], device_id=(to, col), device_id_type=MESH
        ).start()
        return carry

    def second_hop(kind):
        @pl.when(core == kind)
        def _():
            recv1[0] = send1[row]
            pltpu.make_async_copy(away1, away1, r1_sem).wait()
            lax.fori_loop(0, ROWS - 1, hop2, 0)
            pick(row, 0)
            recv2[0] = send2[row]

    second_hop(0)

    @pl.when(core == 0)
    def _():
        hop1(1)

    recv_b[0] = send_b[plane]
    away_b = recv_b.at[pl.ds(1, 3)]
    pltpu.make_async_copy(away_b, away_b, rb_sem).wait()

    zero = jnp.zeros((16, 128), F32)
    sum_z, sum_x, sum_s = (
        recv_b[0, j].astype(F32) + recv_b[1, j].astype(F32) + recv_b[2, j].astype(F32) + recv_b[3, j].astype(F32)
        for j in range(3)
    )
    lane = lax.broadcasted_iota(I32, (16, 128), 1)
    sub = lax.broadcasted_iota(I32, (16, 128), 0)
    low = lane < HP
    mine = lane == sub + 16 * member

    def as_column(k):
        return jnp.sum(jnp.where(mine, jnp.broadcast_to(sum_z[k : k + 1], (16, 128)), 0.0), axis=1, keepdims=True)

    root = jnp.sqrt(as_column(15) / D + EPSILON)
    real = sub < SLOTS
    gate_in = jnp.where(real, sum_z / root, 0.0).astype(BF16).astype(F32)
    value_in = jnp.where(real, sum_x / root, 0.0).astype(BF16)
    step_in = jnp.where(low, as_column(13) / root, as_column(14) / root).astype(BF16).astype(F32)

    for e in range(4):
        for half in range(2):
            rows_e = recv_b[e, 3 + half].astype(F32)
            for d in range(4):
                came[8 * e + 4 * half + d, 0:4, :] = rows_e[4 * d : 4 * d + 4]
    codes = [table[0, ROWS * k + row] for k in range(MOVES)]
    tiles = []
    for code in codes:
        at = (row - (code >> 3)) & (ROWS - 1)
        tiles.append(came[8 * ((plane - (at >> 3)) & 3) + ((member - (at & 7)) & 7)])
    quarter = lane >> 5
    bc_rows = zero
    for k in range(3):
        for m in range(MOVES):
            moved = jnp.broadcast_to(tiles[m][3:4], (16, 128))
            moved = moved if m == k else pltpu.roll(moved, (32 * (m - k)) % 128, 1)
            bc_rows = jnp.where((sub == SLOTS + k) & (quarter == m), moved, bc_rows)
    send_s[...] = jnp.where(real, sum_s / root, bc_rows).astype(BF16)

    def share(j, carry):
        d = far_first(j, 8)
        to = (col + d) & (COLS - 1)
        pltpu.make_async_remote_copy(
            send_s, recv_s.at[d], ss_sem, rs_sem, device_id=(row, to), device_id_type=MESH
        ).start()
        return carry

    lax.fori_loop(0, COLS - 1, share, 0)
    recv_s[0] = send_s[...]

    second_hop(1)

    def wait_pieces(kind):
        @pl.when(core == kind)
        def _():
            some = recv2.at[pl.ds(0, 15)]
            pltpu.make_async_copy(some, some, r2_sem.at[kind]).wait()

        @pl.when(core != kind)
        def _():
            some = recv2.at[pl.ds(0, 16)]
            pltpu.make_async_copy(some, some, r2_sem.at[kind]).wait()

    def with_arrived(i, rows_of):
        rows_i = jnp.concatenate([windows[i], jnp.zeros((3, 128), F32)], axis=0)
        for k in range(MOVES):
            rows_i = jnp.where(sub == slots[k], jnp.broadcast_to(rows_of(k), (16, 128)), rows_i)
        return rows_i

    window = [with_arrived(i, lambda k, i=i: tiles[k][i : i + 1]) for i in range(3)]

    taps_x = cwx[...].astype(F32)
    taps_bc = cwbc[...].astype(F32)
    conv = value_in.astype(F32) * taps_x[3:4]
    for k in range(3):
        conv = conv + window[k] * taps_x[k : k + 1]
    value_act = silu(conv)
    cx_out[0] = window[1][:SLOTS].astype(BF16)
    cx_out[1] = window[2][:SLOTS].astype(BF16)
    cx_out[2] = value_in[:SLOTS]
    head_lanes = lambda ref: jnp.where(low, ref[0], ref[1])
    raw_step = step_in + head_lanes(dtb)
    step = jnp.maximum(raw_step, 0.0) + jnp.log1p(jnp.exp(-jnp.abs(raw_step)))
    decay = jnp.exp(-jnp.exp(head_lanes(alog)) * step)
    grown = step * value_act

    away_s = recv_s.at[pl.ds(1, COLS - 1)]
    pltpu.make_async_copy(away_s, away_s, rs_sem).wait()

    def chunk(c):
        return recv_s[(col - c) & (COLS - 1)]

    for c in range(4):
        joined = []
        for m in range(MOVES):
            rows_m = zero
            for j in range(4):
                other = chunk(4 * c + j).astype(F32)
                other = other if j == m else pltpu.roll(other, (32 * (j - m)) % 128, 1)
                rows_m = jnp.where(quarter == j, other, rows_m)
            joined.append(rows_m)
        window += [
            with_arrived(3 + 4 * k + c, lambda m, k=k: joined[m][SLOTS + k : SLOTS + k + 1]) for k in range(3)
        ]
    act = []
    for c in range(4):
        new = chunk(c)
        lanes = slice(128 * c, 128 * (c + 1))
        conv = new.astype(F32) * taps_bc[3:4, lanes]
        for k in range(3):
            conv = conv + window[3 + 3 * c + k] * taps_bc[k : k + 1, lanes]
        act.append(silu(conv).astype(BF16))
        cbc_out[0, :, lanes] = window[3 + 3 * c + 1][:SLOTS].astype(BF16)
        cbc_out[1, :, lanes] = window[3 + 3 * c + 2][:SLOTS].astype(BF16)
        cbc_out[2, :, lanes] = new[:SLOTS]
    b_in = jnp.concatenate(act[:2], axis=1)
    c_out = jnp.concatenate(act[2:], axis=1)

    qbuf[...] = jnp.zeros_like(qbuf)
    for h in range(8):
        lanes = slice(128 * (h // 4), 128 * (h // 4 + 1))
        qbuf[:, h, lanes] = chunk(4 + h).astype(F32)
    for j in range(4):
        fresh[:, 0, 128 * j : 128 * (j + 1)] = chunk(12 + j).astype(F32)

    def length_of(s):
        request = row * SLOTS + s
        for k in range(MOVES):
            at = (row - (codes[k] >> 3)) & (ROWS - 1)
            request = jnp.where(slots[k] == s, at * SLOTS + ms[codes[k] & 3, at], request)
        return lengths[request]

    line = lax.broadcasted_iota(I32, (PAGE, 512), 0)

    def page(at, s, half):
        length = length_of(s)
        logical = length >> 5
        here = ((logical & (COLS - 1)) == col) & ((logical >> 4) == half)
        offset = jnp.where(here, length & (PAGE - 1), -1)
        return jnp.where(line == offset, fresh[s].astype(F32), pcomb[at].astype(F32)).astype(BF16)

    def own_page(g, carry):
        entry = table[1, g]
        kvn[g] = page(g, entry >> 1, entry & 1)
        return carry

    lax.fori_loop(0, 26, own_page, 0)
    kv_copy = pltpu.make_async_copy(kvn.at[pl.ds(0, 26)], kv_out.at[pl.ds(0, 26)], out_sem.at[0])
    kv_copy.start()

    token = lax.broadcasted_iota(I32, (8, 64), 1)
    position = (token >> 5) * (COLS * PAGE) + col * PAGE + (token & (PAGE - 1))
    head = lax.broadcasted_iota(I32, (8, 128), 0)
    lane8 = lax.broadcasted_iota(I32, (8, 128), 1)

    def attention(s, first, second):
        both = jnp.concatenate([first, second], axis=0)
        scores = nt(qbuf[s].astype(BF16), both[:, :256]) * (HD**-0.5)
        live = position <= length_of(s)
        peak = jnp.max(jnp.where(live, scores, FLOOR), axis=1, keepdims=True)
        weights = jnp.where(live, jnp.exp(scores - peak), 0.0)
        summed = nn(weights.astype(BF16), both[:, 256:])
        summed = jnp.where(head < 4, summed[:, :128], summed[:, 128:])
        rounded = peak.astype(BF16).astype(F32)
        rest = (peak - rounded).astype(BF16).astype(F32)
        stats = jnp.where(lane8 == HP, rounded, jnp.sum(weights, axis=1, keepdims=True))
        stats = jnp.where(lane8 == HP + 1, rest, stats)
        stats = jnp.where(lane8 == HP + 2, peak - rounded - rest, stats)
        return jnp.where(lane8 < HP, summed, stats), jnp.where(lane8 < HP, pltpu.roll(summed, HP, 1), stats)

    for s in range(SLOTS):
        send_a[:, 0, s, :], send_a[:, 1, s, :] = attention(s, kvn[pt[0, s]], kvn[pt[1, s]])
    for s in range(SLOTS, 16):
        send_a[:, 0, s, :] = jnp.zeros((8, 128), F32)
        send_a[:, 1, s, :] = jnp.zeros((8, 128), F32)

    wait_pieces(0)

    def paste_pages(k, carry):
        for p in range(16):
            i = p % 8
            r, l = 16 * (i // 4), 128 * (i % 4)
            pcomb[26 + 2 * k + p // 8, r : r + 16, l : l + 128] = recv2[(row - 2 * p) & (ROWS - 1), k]
        for half in range(2):
            kvn[26 + 2 * k + half] = page(26 + 2 * k + half, ms[k, row], half)
        return carry

    lax.fori_loop(0, MOVES, paste_pages, 0)
    kv_copy2 = pltpu.make_async_copy(kvn.at[pl.ds(26, 8)], kv_out.at[pl.ds(26, 8)], out_sem.at[1])
    kv_copy2.start()
    found = [attention(slots[k], kvn[26 + 2 * k], kvn[27 + 2 * k]) for k in range(MOVES)]
    for h in range(8):
        for half in range(2):
            tile = send_a[h, half]
            for k in range(MOVES):
                tile = jnp.where(sub == slots[k], jnp.broadcast_to(found[k][half][h : h + 1], (16, 128)), tile)
            leave_a[h, half] = tile.astype(BF16)

    def attend(j, carry):
        d = far_first(j, 8)
        to = (col + d) & (COLS - 1)
        pltpu.make_async_remote_copy(
            leave_a.at[to >> 1, to & 1], recv_a.at[d], sa_sem, ra_sem, device_id=(row, to), device_id_type=MESH
        ).start()
        return carry

    lax.fori_loop(0, COLS - 1, attend, 0)
    recv_a[0] = leave_a[col >> 1, col & 1]

    read = zero
    for s in range(SLOTS):
        read = jnp.where(sub == s, nt(c_out, scomb[s]), read)
    columns = jnp.concatenate([grown, decay, jnp.zeros((96, 128), F32)], axis=0).T
    for s in range(SLOTS):
        old = scomb[s].astype(F32)
        new = columns[:, 16 + s : 17 + s] * old + columns[:, s : s + 1] * b_in[s : s + 1].astype(F32)
        stn[s] = new.astype(BF16)
    own_states = pl.ds(0, SLOTS)
    state_copy_out = pltpu.make_async_copy(stn.at[own_states], state_out.at[own_states], out_sem.at[2])
    state_copy_out.start()
    b_dot_c = jnp.sum(b_in.astype(F32) * c_out.astype(F32), axis=1, keepdims=True)
    loads[5].wait()
    loads[6].wait()

    wait_pieces(1)

    def paste_states(k, carry):
        for p in range(16):
            r, l = 16 * (p // 2), 128 * (p % 2)
            scomb[SLOTS + k, r : r + 16, l : l + 128] = recv2[(row - 2 * p - 1) & (ROWS - 1), k]
        return carry

    lax.fori_loop(0, MOVES, paste_states, 0)
    for k in range(MOVES):
        read = jnp.where(sub == slots[k], nt(c_out, scomb[SLOTS + k]), read)
    readout = decay * read + grown * b_dot_c + head_lanes(dskip) * value_act
    gated = (readout * silu(gate_in)).astype(BF16)
    out_terms = nn(gated, wssm_v[...])

    away_a = recv_a.at[pl.ds(1, COLS - 1)]
    pltpu.make_async_copy(away_a, away_a, ra_sem).wait()
    parts = [recv_a[d].astype(F32) for d in range(COLS)]
    peaks = [part[:, HP : HP + 1] + part[:, HP + 1 : HP + 2] + part[:, HP + 2 : HP + 3] for part in parts]
    top = peaks[0]
    for peak in peaks[1:]:
        top = jnp.maximum(top, peak)
    gathered = zero
    for part, peak in zip(parts, peaks):
        gathered = gathered + part * jnp.exp(peak - top)
    attended = jnp.where(real, gathered / gathered[:, HP + 3 : HP + 4], 0.0).astype(BF16)
    out_terms = out_terms + nn(attended[:, :HP], wattn_v[...])
    for c in range(COLS):
        send_o[c] = out_terms[:, 128 * c : 128 * (c + 1)].astype(BF16)

    def project(j, carry):
        d = far_first(j, 8)
        to = (col + d) & (COLS - 1)
        pltpu.make_async_remote_copy(
            send_o.at[to], recv_o.at[d], so_sem, ro_sem, device_id=(row, to), device_id_type=MESH
        ).start()
        return carry

    lax.fori_loop(0, COLS - 1, project, 0)
    recv_o[0] = send_o[col]

    lanes = lax.broadcasted_iota(I32, (128, 128), 1)
    rows_b = lax.broadcasted_iota(I32, (16, 256), 0)
    for k in range(MOVES):
        up = jnp.sum(jnp.where(lanes == slots[k], columns, 0.0), axis=1, keepdims=True)
        down_by = jnp.sum(jnp.where(lanes == slots[k] + 16, columns, 0.0), axis=1, keepdims=True)
        b_row = jnp.sum(jnp.where(rows_b == slots[k], b_in.astype(F32), 0.0), axis=0, keepdims=True)
        stn[SLOTS + k] = (down_by * scomb[SLOTS + k].astype(F32) + up * b_row).astype(BF16)
    new_states = pl.ds(SLOTS, MOVES)
    state_copy2 = pltpu.make_async_copy(stn.at[new_states], state_out.at[new_states], out_sem.at[3])
    state_copy2.start()

    away_o = recv_o.at[pl.ds(1, COLS - 1)]
    pltpu.make_async_copy(away_o, away_o, ro_sem).wait()
    mixed = zero
    for d in range(COLS):
        mixed = mixed + recv_o[d].astype(F32)
    mixed_out[...] = mixed[:SLOTS].astype(BF16)

    sent1 = send1.at[pl.ds(0, ROWS - 1)]
    pltpu.make_async_copy(sent1, sent1, s1_sem).wait()
    sent2 = send2.at[pl.ds(0, ROWS - 1)]
    pltpu.make_async_copy(sent2, sent2, s2_sem).wait()
    sent_r = send_r.at[pl.ds(0, 7)]
    pltpu.make_async_copy(sent_r, sent_r, sr_sem).wait()
    sent_b = send_b.at[pl.ds(0, 3)]
    pltpu.make_async_copy(sent_b, sent_b, sb_sem).wait()
    for sem, ref in ((ss_sem, recv_s), (sa_sem, recv_a), (so_sem, send_o)):
        sent = ref.at[pl.ds(0, COLS - 1)]
        pltpu.make_async_copy(sent, sent, sem).wait()
    for copy in (kv_copy, kv_copy2, state_copy_out, state_copy2):
        copy.wait()


def emit_kernel(ms, pt, *refs):
    made, out, held, sem = refs[:5], refs[5:10], refs[10:15], refs[15]
    row = lax.axis_index("rows")
    ready = list(held)
    ready[0] = held[0].at[pl.ds(0, 26)]
    ready[1] = held[1].at[pl.ds(0, SLOTS)]
    reads = [pltpu.make_async_copy(made[i], held[i], sem.at[i]) for i in range(5)]
    writes = [pltpu.make_async_copy(ready[i], out[i], sem.at[5 + i]) for i in range(5)]
    for read in reads:
        read.start()
    for i in (2, 3, 4, 0, 1):
        reads[i].wait()
        for k in range(MOVES):
            slot = ms[k, row]
            if i == 0:
                held[0][pt[0, slot]] = held[0][26 + 2 * k]
                held[0][pt[1, slot]] = held[0][27 + 2 * k]
            if i == 1:
                held[1][slot] = held[1][SLOTS + k]
        writes[i].start()
    for write in writes:
        write.wait()


def local(
    tokens, arrival, cache_lengths, move_slot, move_target, page_table, kv_pool, ssm_state, conv_x, conv_bc,
    norm_gain, weight_z, weight_x, weight_dt, weight_bc, weight_qkv, conv_weight_x, conv_weight_bc,
    dt_bias, a_log, d_skip, weight_ssm_out, weight_attn_out,
):
    vmem = pl.BlockSpec(memory_space=pltpu.VMEM)
    smem = pl.BlockSpec(memory_space=pltpu.SMEM)
    anywhere = pl.BlockSpec(memory_space=pl.ANY)
    ms, mt = move_slot.T, move_target.T
    pt = page_table.reshape(SLOTS, 2).T
    dma = pltpu.SemaphoreType.DMA
    results = (
        jax.ShapeDtypeStruct((26, PAGE, 512), BF16),
        jax.ShapeDtypeStruct((SLOTS, 128, NS), BF16),
        jax.ShapeDtypeStruct((SLOTS, 128), BF16),
        jax.ShapeDtypeStruct((3, SLOTS, 128), BF16),
        jax.ShapeDtypeStruct((3, SLOTS, 512), BF16),
    )
    tile = lambda *lead: pltpu.VMEM((*lead, 16, 128), BF16)
    made = pl.pallas_call(
        mixer_kernel,
        out_shape=(
            jax.ShapeDtypeStruct((34, PAGE, 512), BF16),
            jax.ShapeDtypeStruct((SLOTS + MOVES, 128, NS), BF16),
            *results[2:],
        ),
        in_specs=[smem] * 7 + [vmem] * 9 + [anywhere] * 9,
        out_specs=(anywhere, anywhere, vmem, vmem, vmem),
        scratch_shapes=[
            tile(ROWS, MOVES),
            tile(ROWS, MOVES),
            tile(ROWS, MOVES),
            tile(ROWS, MOVES),
            pltpu.VMEM((34, PAGE, 512), BF16),
            pltpu.VMEM((SLOTS + MOVES, 128, NS), BF16),
            pltpu.VMEM((34, PAGE, 512), BF16),
            pltpu.VMEM((SLOTS + MOVES, 128, NS), BF16),
            pltpu.VMEM((16, 8, 128), F32),
            pltpu.VMEM((8, 16, 128), F32),
            pltpu.VMEM((4, 32, 128), F32),
            pltpu.VMEM((ROWS, 8, 128), F32),
            pltpu.VMEM((8, 128), I32),
            pltpu.SMEM((8, 128), I32),
            tile(8, 13),
            tile(8, 13),
            tile(4, 5),
            tile(4, 5),
            tile(),
            tile(COLS),
            pltpu.VMEM((16, 8, 256), F32),
            pltpu.VMEM((16, 1, 512), F32),
            pltpu.VMEM((8, 2, 16, 128), F32),
            tile(8, 2),
            tile(COLS),
            tile(COLS),
            tile(COLS),
            pltpu.VMEM((64, 416), BF16),
            pltpu.VMEM((64, 128), BF16),
            pltpu.VMEM((64, 128), BF16),
            pltpu.VMEM((2, 64, 128), BF16),
            pltpu.VMEM((128, D), BF16),
            pltpu.VMEM((64, D), BF16),
        ]
        + [dma] * 3
        + [dma((2,))]
        + [dma] * 10
        + [dma((9,)), dma, dma((4,))],
        compiler_params=pltpu.CompilerParams(
            collective_id=0, has_side_effects=True, vmem_limit_bytes=60 * 1024 * 1024
        ),
        name="mixer",
    )(
        ms, mt, cache_lengths, pt, dt_bias, a_log, d_skip,
        ms, mt, arrival.reshape(1, 416), norm_gain.reshape(1, 64), weight_dt.T, conv_weight_x, conv_weight_bc,
        conv_x.transpose(1, 0, 2), conv_bc.transpose(1, 0, 2),
        tokens.T, weight_z, weight_x, weight_bc, weight_qkv, weight_ssm_out, weight_attn_out,
        kv_pool.reshape(26, PAGE, 512), ssm_state.reshape(SLOTS, 128, NS),
    )
    kv_next, state_next, mixed, cx, cbc = pl.pallas_call(
        emit_kernel,
        out_shape=results,
        in_specs=[smem] * 2 + [anywhere] * 5,
        out_specs=(anywhere,) * 5,
        scratch_shapes=[pltpu.VMEM(m.shape, m.dtype) for m in made] + [dma((10,))],
        name="emit",
    )(ms, pt, *made)
    return (
        mixed,
        state_next.reshape(SLOTS, 2, HP, NS),
        cx.transpose(1, 0, 2),
        cbc.transpose(1, 0, 2),
        kv_next.reshape(26, 1, PAGE, 512),
    )


def solution(mesh):
    in_specs = (
        P(None, "rows"), P(), P(), P(), P(), P("rows", "cols", None, None), P("rows", "cols", None, None),
        P("rows", "cols", None, None), P("rows", None, "cols"), P("rows", None, None), P("rows"),
        P("rows", "cols"), P("rows", "cols"), P("rows", "cols"), P("rows", None), P("rows", None),
        P(None, "cols"), P(), P("cols"), P("cols"), P("cols"), P("cols", None), P("cols", None),
    )
    out_specs = (
        P("rows", "cols"),
        P("rows", "cols", None, None),
        P("rows", None, "cols"),
        P("rows", None, None),
        P("rows", "cols", None, None),
    )
    return jax.shard_map(local, mesh=mesh, in_specs=in_specs, out_specs=out_specs, check_vma=False)
```
